32 devices in a mesh: grp: 4 (over z), dom: 8 (over y, x, core).
Axes of the slice: x: 2, y: 2, z: 4, core: 2. Of those that a mesh axis runs over, the one named last changes fastest.
Arguments:
- leaf_load: bfloat16 [8, 4, 1024, 128], P('dom', 'grp'), may hold values from -6 to 6
- leaf_map: bfloat16 [8, 4, 1024, 1024], P('dom', 'grp'), may hold values from -0.1875 to 0.1875
- group_map: bfloat16 [8, 4096, 4096], P('dom', 'grp'), may hold values from -0.09375 to 0.09375
- node_index: int32 [8, 4, 1024], P('dom', 'grp'), may hold values from 0 to 4095, as said below
- west_coupling: float32 [8, 256, 256], P('dom'), may hold values from -1.5 to 1.5
- east_coupling: float32 [8, 256, 256], P('dom'), may hold values from -1.5 to 1.5
Outputs:
- leaf_solution: bfloat16 [8, 4, 1024, 128], P('dom', 'grp')
The draws below stay inside these ranges and needn't reach their ends.
Inputs may be any that keep to these rules, and one draw needn't show every extreme that they name: `node_index`: each leaf's list names 1024 different interface nodes of its group.
All inputs are finite; a program needn't handle non-finite values.
Results may differ from the reference program's by a relative error of at most 0.015.
Values may be sent and summed in bfloat16 or wider, within the bound.
A program may use at most 128 MiB of HBM per device.

```python
import jax
import jax.numpy as jnp
from jax import lax

B = 1024
IF = 4096
NB = 256
R = 128
LEAVES = 4
DOMS = 8


def draw_node_index(key, part):
    subkeys = jax.random.split(key, DOMS * LEAVES)
    chosen = jax.vmap(lambda single: jax.random.permutation(single, IF)[:B])(subkeys)
    return chosen.reshape(DOMS, LEAVES, B).astype(jnp.int32)


def block_levels(stream_key, extent, cuts, least, largest):
    def one(position, parts):
        steps = jax.random.uniform(jax.random.fold_in(jax.random.fold_in(stream_key, 6), position), (parts,), jnp.float32, least / len(cuts), largest / len(cuts))
        return jnp.repeat(jnp.exp(steps), extent[position] // parts).reshape((-1,) + (1,) * (len(extent) - position - 1))

    gain = one(*cuts[0])
    for cut in cuts[1:]:
        gain = gain * one(*cut)
    return gain


def normal_values(stream_key, shape, width, bound, shards=(), dtype=jnp.bfloat16):
    entries = width * jax.random.normal(stream_key, shape, jnp.float32)
    if shards:
        entries = entries * block_levels(stream_key, shape, shards, -0.22, 0.18)
    return jnp.clip(entries, -bound, bound).astype(dtype)


def setup_inputs(seed: int = 0) -> dict:
    key_of = jax.random.split(jax.random.key(seed), 7)
    leaf_load = normal_values(key_of[0], (DOMS, LEAVES, B, R), 1.0, 6.0, ((0, 8), (1, 4)))
    leaf_map = normal_values(key_of[1], (DOMS, LEAVES, B, B), B ** -0.5, 0.1875, ((0, 8), (1, 4)))
    group_map = normal_values(key_of[2], (DOMS, IF, IF), IF ** -0.5, 0.09375, ((0, 8), (1, 4)))
    node_index = draw_node_index(jax.random.fold_in(key_of[6], 71), 0)
    west_coupling = normal_values(key_of[4], (DOMS, NB, NB), (NB * NB * 10 // (9 * IF)) ** -0.5, 1.5, ((0, 8),), jnp.float32)
    east_coupling = normal_values(key_of[5], (DOMS, NB, NB), (NB * NB * 10 // (9 * IF)) ** -0.5, 1.5, ((0, 8),), jnp.float32)
    return dict(leaf_load=leaf_load, leaf_map=leaf_map, group_map=group_map, node_index=node_index, west_coupling=west_coupling, east_coupling=east_coupling)


def reference(leaf_load, leaf_map, group_map, node_index, west_coupling, east_coupling):
    exact_mode = lax.Precision.HIGHEST
    stride = IF // NB
    initial_rows = []
    for domain in range(DOMS):
        contrib = jnp.einsum("lij,ljr->lir", leaf_map[domain].astype(jnp.float32), leaf_load[domain].astype(jnp.float32)).astype(jnp.bfloat16)
        summed = jnp.zeros((IF, R), jnp.float32).at[node_index[domain].reshape(-1)].add(contrib.reshape(-1, R).astype(jnp.float32))
        initial_rows.append(jnp.dot(group_map[domain], summed.astype(jnp.bfloat16), preferred_element_type=jnp.float32))
    carried = jnp.zeros((NB, R), jnp.float32)
    swept_rows = []
    for domain in range(DOMS):
        coupled = jnp.dot(west_coupling[domain], carried, precision=exact_mode)
        columns = group_map[domain][:, 0::stride].astype(jnp.float32)
        current = initial_rows[domain] + jnp.dot(columns, coupled, precision=exact_mode)
        swept_rows.append(current)
        carried = current[1::stride]
    carried = jnp.zeros((NB, R), jnp.float32)
    final_rows = [None] * DOMS
    for domain in range(DOMS - 1, -1, -1):
        coupled = jnp.dot(east_coupling[domain], carried, precision=exact_mode)
        columns = group_map[domain][:, 1::stride].astype(jnp.float32)
        current = swept_rows[domain] + jnp.dot(columns, coupled, precision=exact_mode)
        final_rows[domain] = current
        carried = current[0::stride]
    outputs = []
    for domain in range(DOMS):
        solution_rows = final_rows[domain].astype(jnp.bfloat16)
        picked = solution_rows[node_index[domain]]
        result = jnp.einsum("lbi,lbr->lir", leaf_map[domain].astype(jnp.float32), picked.astype(jnp.float32)) + leaf_load[domain].astype(jnp.float32)
        outputs.append(result.astype(jnp.bfloat16))
    return jnp.stack(outputs)
```

```python
import functools

import jax
import jax.numpy as jnp
from jax import lax
from jax.experimental import pallas as pl
from jax.experimental.pallas import tpu as pltpu
from jax.sharding import PartitionSpec as P

MESH = pl.DeviceIdType.MESH
BF = jnp.bfloat16
F32 = jnp.float32


def dot(a, b):
    return jnp.dot(a, b, preferred_element_type=F32)


def flip(d, mask):
    out = d
    bit = 1
    while bit <= mask:
        if mask & bit:
            out = out + (1 - 2 * (lax.div(d, bit) % 2)) * bit
        bit *= 2
    return out


def subsets(bits):
    found = [0]
    for bit in bits:
        found += [m | bit for m in found]
    return found


def kernel(
    n, doms,
    lm_ref, ll_ref, g_hbm, idx_ref, wc_ref, ec_ref, out_ref,
    g, contrib, idx_all, loads, loads_b, sel, gface, gsel, maps, faces, ebuf, wbuf, swept, init, sol, pt, lmt, picked,
    g_sem, i_s, i_r, c_s, c_r, m_s, m_r, f_s, f_r, o_s, o_r, ms, mr, fs, fr_,
):
    z = lax.axis_index("grp")
    d = lax.axis_index("dom")
    rows, interface = g.shape
    nodes, cols = ll_ref.shape
    face = wc_ref.shape[0]
    stride = interface // face
    fr = rows // stride
    bits = []
    while (1 << len(bits)) < doms:
        bits.append(1 << len(bits))
    tile = 512

    load_g = pltpu.make_async_copy(g_hbm, g, g_sem)
    load_g.start()
    barrier = pltpu.get_barrier_semaphore()
    for o in range(1, n):
        pl.semaphore_signal(barrier, inc=1, device_id={"grp": (z + o) % n}, device_id_type=MESH)
    for bit in bits:
        pl.semaphore_signal(barrier, inc=1, device_id={"dom": flip(d, bit)}, device_id_type=MESH)

    contrib[z] = dot(lm_ref[...], ll_ref[...]).astype(BF)
    idx_all[z] = idx_ref[...]
    pl.semaphore_wait(barrier, n - 1 + len(bits))

    def to_group(ref, ss, rs):
        made = []
        for o in range(1, n):
            made.append(pltpu.make_async_remote_copy(
                src_ref=ref, dst_ref=ref, send_sem=ss.at[o], recv_sem=rs.at[o],
                device_id={"grp": (z + o) % n}, device_id_type=MESH))
        return made

    def start(copies):
        for c in copies:
            c.start()

    def wait(copies):
        for c in copies:
            c.wait()

    i_copies = to_group(idx_all.at[z], i_s, i_r)
    c_copies = to_group(contrib.at[z], c_s, c_r)
    start(i_copies)
    start(c_copies)

    half = interface // 2
    hf = face // 2
    a = lax.broadcasted_iota(jnp.int32, (half, face), 0)
    b = lax.broadcasted_iota(jnp.int32, (half, face), 1)
    want = jnp.where(b < hf, b * stride, (b - hf) * stride + 1)
    sel[...] = jnp.where(a == want, 1.0, 0.0).astype(BF)
    a = lax.broadcasted_iota(jnp.int32, (2 * fr, rows), 0)
    b = lax.broadcasted_iota(jnp.int32, (2 * fr, rows), 1)
    want = jnp.where(a < fr, a * stride, (a - fr) * stride + 1)
    pick_rows = jnp.where(b == want, 1.0, 0.0).astype(BF)

    load_g.wait()
    step = min(256, rows)

    @pl.loop(0, rows // step)
    def _(i):
        r0 = pl.multiple_of(i * step, step)
        for c in range(2):
            got = dot(g[pl.ds(r0, step), c * half:(c + 1) * half], sel[...]).astype(BF)
            gsel[pl.ds(r0, step), c * hf:(c + 1) * hf] = got[:, :hf]
            gsel[pl.ds(r0, step), face + c * hf:face + (c + 1) * hf] = got[:, hf:]

    ff = dot(pick_rows, gsel[...]).astype(BF)

    def split(x):
        high = x.astype(BF)
        return high, (x - high.astype(F32)).astype(BF)

    wc_h, wc_l = split(wc_ref[...])
    ec_h, ec_l = split(ec_ref[...])
    forward = dot(ff[:, :face], wc_h) + dot(ff[:, :face], wc_l)
    backward = dot(ff[:fr, face:], ec_h) + dot(ff[:fr, face:], ec_l)
    z0 = pl.multiple_of(z * fr, fr)
    maps[d, 0, pl.ds(z0, fr), :] = forward[:fr].astype(BF)
    maps[d, 1, pl.ds(z0, fr), :] = forward[fr:].astype(BF)
    maps[d, 2, pl.ds(z0, fr), :] = backward.astype(BF)
    m_copies = to_group(maps.at[d, :, pl.ds(z0, fr), :], m_s, m_r)
    start(m_copies)

    @pl.loop(0, interface // tile)
    def _(i):
        c0 = pl.multiple_of(i * tile, tile)
        gface[:, pl.ds(c0, tile)] = dot(pick_rows, g[:, pl.ds(c0, tile)]).astype(BF)

    def add_loads(block, first):
        @pl.loop(0, interface // tile)
        def _(i):
            r0 = pl.multiple_of(i * tile, tile)
            place = lax.broadcasted_iota(jnp.int32, (tile, 128), 0) + r0
            hot = jnp.concatenate([
                jnp.where(place == idx_all[block, pl.ds(r, 1), :], 1.0, 0.0).astype(BF)
                for r in range(nodes // 128)], axis=1)
            part = dot(hot, contrib[block])
            if first:
                loads[pl.ds(r0, tile), :] = part
            else:
                loads[pl.ds(r0, tile), :] += part

    def spread(ref, part, order, ss, rs):
        done, steps = [], []
        for bit in order:
            steps.append([pltpu.make_async_remote_copy(
                src_ref=ref.at[flip(d, m), part], dst_ref=ref.at[flip(d, m), part],
                send_sem=ss.at[part, m | bit], recv_sem=rs.at[part, m | bit],
                device_id={"dom": flip(d, bit)}, device_id_type=MESH) for m in subsets(done)])
            done.append(bit)
        return steps

    order_a = bits[::-1]
    order_b = order_a if len(bits) < 3 else [order_a[1], order_a[0]] + order_a[2:]
    map_steps = [spread(maps, p, (order_a, order_b, order_a)[p], ms, mr) for p in range(3)]
    face_steps = [spread(faces, p, (order_a, order_b)[p], fs, fr_) for p in range(2)]

    wait(i_copies)
    add_loads(z, True)
    wait(m_copies)
    for s in map_steps:
        start(s[0])

    turned = jnp.transpose(idx_ref[...])
    for r in range(nodes // 128):
        column = turned[:, r:r + 1]

        @pl.loop(0, interface // tile)
        def _(i):
            c0 = pl.multiple_of(i * tile, tile)
            place = lax.broadcasted_iota(jnp.int32, (128, tile), 1) + c0
            pt[r * 128:(r + 1) * 128, pl.ds(c0, tile)] = jnp.where(place == column, 1.0, 0.0).astype(BF)

    lmt[...] = jnp.transpose(lm_ref[...])

    for k in range(1, n):
        c_copies[k - 1].wait()
        add_loads((z - k + n) % n, False)
        if k < len(bits):
            for s in map_steps:
                wait(s[k - 1])
                start(s[k])
    for k in range(n, len(bits)):
        for s in map_steps:
            wait(s[k - 1])
            start(s[k])

    loads_b[...] = loads[...].astype(BF)
    here = dot(gface[...], loads_b[...]).astype(BF)
    faces[d, 0, pl.ds(z0, fr), :] = here[:fr]
    faces[d, 1, pl.ds(z0, fr), :] = here[fr:]
    f_copies = to_group(faces.at[d, :, pl.ds(z0, fr), :], f_s, f_r)
    start(f_copies)
    wait(f_copies)
    for s in face_steps:
        start(s[0])

    @pl.loop(0, rows // step)
    def _(i):
        r0 = pl.multiple_of(i * step, step)
        init[pl.ds(r0, step), :] = dot(g[pl.ds(r0, step), :], loads_b[...])

    for k in range(1, len(bits)):
        for s in face_steps:
            wait(s[k - 1])
            start(s[k])
    for s in map_steps:
        wait(s[-1])
    for s in face_steps:
        wait(s[-1])

    ebuf[0] = jnp.zeros((face, cols), BF)
    ebuf[1] = faces[0, 1]
    first = faces[0, 1].astype(F32)

    def ahead(j, carry):
        both = maps[j, pl.ds(0, 2)].reshape(2 * face, face)
        got = dot(both, ebuf[j])
        swept[j] = got[:face] + faces[j, 0].astype(F32)
        ebuf[j + 1] = (got[face:] + faces[j, 1].astype(F32)).astype(BF)
        return carry

    lax.fori_loop(1, doms, ahead, 0)
    wbuf[doms] = jnp.zeros((face, cols), BF)

    def back(t, carry):
        j = doms - 1 - t
        wbuf[j] = (swept[j] + dot(maps[j, 2], wbuf[j + 1])).astype(BF)
        return carry

    lax.fori_loop(0, doms - 1, back, 0)
    inc = ebuf[d]
    outgoing = wbuf[d + 1]
    vw = (dot(wc_h, inc) + dot(wc_l, inc)).astype(BF)
    ve = (dot(ec_h, outgoing) + dot(ec_l, outgoing)).astype(BF)
    sol[z] = (init[...] + dot(gsel[...], jnp.concatenate([vw, ve], axis=0))).astype(BF)
    o_copies = to_group(sol.at[z], o_s, o_r)
    start(o_copies)

    def add_picked(block):
        c0 = pl.multiple_of(block * rows, rows)
        return dot(pt[:, pl.ds(c0, rows)], sol[block])

    picked[...] = add_picked(z)
    for k in range(1, n):
        o_copies[k - 1].wait()
        picked[...] += add_picked((z - k + n) % n)
    out_ref[...] = (dot(lmt[...], picked[...].astype(BF)) + ll_ref[...].astype(F32)).astype(BF)


def solution(mesh):
    n, doms = mesh.shape["grp"], mesh.shape["dom"]

    def on_device(leaf_load, leaf_map, group_map, node_index, west_coupling, east_coupling):
        nodes, cols = leaf_load.shape[2:]
        rows, interface = group_map.shape[1:]
        face = west_coupling.shape[1]
        fr = rows // (interface // face)
        vm = pl.BlockSpec(memory_space=pltpu.VMEM)
        dma = pltpu.SemaphoreType.DMA
        out = pl.pallas_call(
            functools.partial(kernel, n, doms),
            out_shape=jax.ShapeDtypeStruct((nodes, cols), BF),
            in_specs=[vm, vm, pl.BlockSpec(memory_space=pl.ANY), vm, vm, vm],
            out_specs=vm,
            scratch_shapes=[
                pltpu.VMEM((rows, interface), BF),
                pltpu.VMEM((n, nodes, cols), BF),
                pltpu.VMEM((n, nodes // 128, 128), jnp.int32),
                pltpu.VMEM((interface, cols), F32),
                pltpu.VMEM((interface, cols), BF),
                pltpu.VMEM((interface // 2, face), BF),
                pltpu.VMEM((2 * fr, interface), BF),
                pltpu.VMEM((rows, 2 * face), BF),
                pltpu.VMEM((doms, 3, face, face), BF),
                pltpu.VMEM((doms, 2, face, cols), BF),
                pltpu.VMEM((doms + 1, face, cols), BF),
                pltpu.VMEM((doms + 1, face, cols), BF),
                pltpu.VMEM((doms, face, cols), F32),
                pltpu.VMEM((rows, cols), F32),
                pltpu.VMEM((n, rows, cols), BF),
                pltpu.VMEM((nodes, interface), BF),
                pltpu.VMEM((nodes, nodes), BF),
                pltpu.VMEM((nodes, cols), F32),
                dma, dma((n,)), dma((n,)), dma((n,)), dma((n,)), dma((n,)), dma((n,)),
                dma((n,)), dma((n,)), dma((n,)), dma((n,)),
                dma((3, doms)), dma((3, doms)), dma((2, doms)), dma((2, doms)),
            ],
            compiler_params=pltpu.CompilerParams(
                collective_id=0, has_side_effects=True, vmem_limit_bytes=60 * 1024 * 1024
            ),
            cost_estimate=pl.CostEstimate(flops=10**10, bytes_accessed=11 * 10**6, transcendentals=0),
        )(
            leaf_map[0, 0], leaf_load[0, 0], group_map[0], node_index.reshape(nodes // 128, 128),
            west_coupling[0], east_coupling[0],
        )
        return out[None, None]

    return jax.shard_map(
        on_device,
        mesh=mesh,
        in_specs=(
            P("dom", "grp", None, None),
            P("dom", "grp", None, None),
            P("dom", "grp", None),
            P("dom", "grp", None),
            P("dom", None, None),
            P("dom", None, None),
        ),
        out_specs=P("dom", "grp", None, None),
        check_vma=False,
    )
```

```python
import functools

import jax
import jax.numpy as jnp
from jax import lax
from jax.experimental import pallas as pl
from jax.experimental.pallas import tpu as pltpu
from jax.sharding import PartitionSpec as P

MESH = pl.DeviceIdType.MESH
BF = jnp.bfloat16
F32 = jnp.float32


def dot(a, b):
    return jnp.dot(a, b, preferred_element_type=F32)


def flip(d, mask):
    out = d
    bit = 1
    while bit <= mask:
        if mask & bit:
            out = out + (1 - 2 * (lax.div(d, bit) % 2)) * bit
        bit *= 2
    return out


def subsets(bits):
    found = [0]
    for bit in bits:
        found += [m | bit for m in found]
    return found


def kernel(
    n, doms,
    lm_ref, ll_ref, g_hbm, idx_ref, wc_ref, ec_ref, out_ref,
    g, contrib, idx_all, loads, loads_b, sel, gface, gsel, maps, faces, ebuf, wbuf, swept, init, sol, pt, lmt, picked, plast,
    g_sem, i_s, i_r, c_s, c_r, m_s, m_r, f_s, f_r, o_s, o_r, ms, mr, fs, fr_,
):
    z = lax.axis_index("grp")
    d = lax.axis_index("dom")
    rows, interface = g.shape
    nodes, cols = ll_ref.shape
    face = wc_ref.shape[0]
    stride = interface // face
    fr = rows // stride
    bits = []
    while (1 << len(bits)) < doms:
        bits.append(1 << len(bits))
    tile = 512

    load_g = pltpu.make_async_copy(g_hbm, g, g_sem)
    load_g.start()
    barrier = pltpu.get_barrier_semaphore()
    for o in range(1, n):
        pl.semaphore_signal(barrier, inc=1, device_id={"grp": (z + o) % n}, device_id_type=MESH)
    for bit in bits:
        pl.semaphore_signal(barrier, inc=1, device_id={"dom": flip(d, bit)}, device_id_type=MESH)

    contrib[z] = dot(lm_ref[...], ll_ref[...]).astype(BF)
    idx_all[z] = idx_ref[...]
    pl.semaphore_wait(barrier, n - 1 + len(bits))

    def to_group(ref, ss, rs):
        made = []
        for o in range(1, n):
            made.append(pltpu.make_async_remote_copy(
                src_ref=ref, dst_ref=ref, send_sem=ss.at[o], recv_sem=rs.at[o],
                device_id={"grp": (z + o) % n}, device_id_type=MESH))
        return made

    def start(copies):
        for c in copies:
            c.start()

    def wait(copies):
        for c in copies:
            c.wait()

    i_copies = to_group(idx_all.at[z], i_s, i_r)
    c_copies = to_group(contrib.at[z], c_s, c_r)
    start(i_copies)
    start(c_copies)

    half = interface // 2
    hf = face // 2
    a = lax.broadcasted_iota(jnp.int32, (half, face), 0)
    b = lax.broadcasted_iota(jnp.int32, (half, face), 1)
    want = jnp.where(b < hf, b * stride, (b - hf) * stride + 1)
    sel[...] = jnp.where(a == want, 1.0, 0.0).astype(BF)
    a = lax.broadcasted_iota(jnp.int32, (2 * fr, rows), 0)
    b = lax.broadcasted_iota(jnp.int32, (2 * fr, rows), 1)
    want = jnp.where(a < fr, a * stride, (a - fr) * stride + 1)
    pick_rows = jnp.where(b == want, 1.0, 0.0).astype(BF)

    load_g.wait()
    step = min(256, rows)

    @pl.loop(0, rows // step)
    def _(i):
        r0 = pl.multiple_of(i * step, step)
        for c in range(2):
            got = dot(g[pl.ds(r0, step), c * half:(c + 1) * half], sel[...]).astype(BF)
            gsel[pl.ds(r0, step), c * hf:(c + 1) * hf] = got[:, :hf]
            gsel[pl.ds(r0, step), face + c * hf:face + (c + 1) * hf] = got[:, hf:]

    ff = dot(pick_rows, gsel[...]).astype(BF)

    def split(x):
        high = x.astype(BF)
        return high, (x - high.astype(F32)).astype(BF)

    wc_h, wc_l = split(wc_ref[...])
    ec_h, ec_l = split(ec_ref[...])
    forward = dot(ff[:, :face], wc_h) + dot(ff[:, :face], wc_l)
    backward = dot(ff[:fr, face:], ec_h) + dot(ff[:fr, face:], ec_l)
    z0 = pl.multiple_of(z * fr, fr)
    maps[d, 0, pl.ds(z0, fr), :] = forward[:fr].astype(BF)
    maps[d, 1, pl.ds(z0, fr), :] = forward[fr:].astype(BF)
    maps[d, 2, pl.ds(z0, fr), :] = backward.astype(BF)
    m_copies = to_group(maps.at[d, :, pl.ds(z0, fr), :], m_s, m_r)
    start(m_copies)

    @pl.loop(0, interface // tile)
    def _(i):
        c0 = pl.multiple_of(i * tile, tile)
        gface[:, pl.ds(c0, tile)] = dot(pick_rows, g[:, pl.ds(c0, tile)]).astype(BF)

    def one_hot(block, r0):
        place = lax.broadcasted_iota(jnp.int32, (tile, 128), 0) + r0
        return jnp.concatenate([
            jnp.where(place == idx_all[block, pl.ds(r, 1), :], 1.0, 0.0).astype(BF)
            for r in range(nodes // 128)], axis=1)

    def add_loads(block, first):
        @pl.loop(0, interface // tile)
        def _(i):
            r0 = pl.multiple_of(i * tile, tile)
            part = dot(one_hot(block, r0), contrib[block])
            if first:
                loads[pl.ds(r0, tile), :] = part
            else:
                loads[pl.ds(r0, tile), :] += part

    def spread(ref, part, order, ss, rs):
        done, steps = [], []
        for bit in order:
            steps.append([pltpu.make_async_remote_copy(
                src_ref=ref.at[flip(d, m), part], dst_ref=ref.at[flip(d, m), part],
                send_sem=ss.at[part, m | bit], recv_sem=rs.at[part, m | bit],
                device_id={"dom": flip(d, bit)}, device_id_type=MESH) for m in subsets(done)])
            done.append(bit)
        return steps

    order_a = bits[::-1]
    order_b = order_a if len(bits) < 3 else [order_a[1], order_a[0]] + order_a[2:]
    map_steps = [spread(maps, p, (order_a, order_b, order_a)[p], ms, mr) for p in range(3)]
    face_steps = [spread(faces, p, (order_a, order_b)[p], fs, fr_) for p in range(2)]

    wait(i_copies)
    add_loads(z, True)
    wait(m_copies)
    for s in map_steps:
        start(s[0])

    turned = jnp.transpose(idx_ref[...])
    for r in range(nodes // 128):
        column = turned[:, r:r + 1]

        @pl.loop(0, interface // tile)
        def _(i):
            c0 = pl.multiple_of(i * tile, tile)
            place = lax.broadcasted_iota(jnp.int32, (128, tile), 1) + c0
            pt[r * 128:(r + 1) * 128, pl.ds(c0, tile)] = jnp.where(place == column, 1.0, 0.0).astype(BF)

    lmt[...] = jnp.transpose(lm_ref[...])

    last = (z + 1) % n
    gp = jnp.zeros((2 * fr, nodes), F32)

    def prepare(i, gp):
        r0 = pl.multiple_of(i * tile, tile)
        hot = one_hot(last, r0)
        plast[pl.ds(r0, tile), :] = hot
        return gp + dot(gface[:, pl.ds(r0, tile)], hot)

    gp = lax.fori_loop(0, interface // tile, prepare, gp).astype(BF)

    for k in range(1, n - 1):
        c_copies[k - 1].wait()
        add_loads((z - k + n) % n, False)
        if k < len(bits):
            for s in map_steps:
                wait(s[k - 1])
                start(s[k])
    for k in range(n - 1, len(bits)):
        for s in map_steps:
            wait(s[k - 1])
            start(s[k])

    here = dot(gface[...], loads[...].astype(BF))
    c_copies[n - 2].wait()
    here = (here + dot(gp, contrib[last])).astype(BF)
    faces[d, 0, pl.ds(z0, fr), :] = here[:fr]
    faces[d, 1, pl.ds(z0, fr), :] = here[fr:]
    f_copies = to_group(faces.at[d, :, pl.ds(z0, fr), :], f_s, f_r)
    start(f_copies)

    @pl.loop(0, interface // tile)
    def _(i):
        r0 = pl.multiple_of(i * tile, tile)
        loads_b[pl.ds(r0, tile), :] = (loads[pl.ds(r0, tile), :] + dot(plast[pl.ds(r0, tile), :], contrib[last])).astype(BF)

    wait(f_copies)
    for s in face_steps:
        start(s[0])

    @pl.loop(0, rows // step)
    def _(i):
        r0 = pl.multiple_of(i * step, step)
        init[pl.ds(r0, step), :] = dot(g[pl.ds(r0, step), :], loads_b[...])

    for k in range(1, len(bits)):
        for s in face_steps:
            wait(s[k - 1])
            start(s[k])
    for s in map_steps:
        wait(s[-1])
    for s in face_steps:
        wait(s[-1])

    ebuf[0] = jnp.zeros((face, cols), BF)
    ebuf[1] = faces[0, 1]
    first = faces[0, 1].astype(F32)

    def ahead(j, carry):
        both = maps[j, pl.ds(0, 2)].reshape(2 * face, face)
        got = dot(both, ebuf[j])
        swept[j] = got[:face] + faces[j, 0].astype(F32)
        ebuf[j + 1] = (got[face:] + faces[j, 1].astype(F32)).astype(BF)
        return carry

    lax.fori_loop(1, doms, ahead, 0, unroll=True)
    wbuf[doms] = jnp.zeros((face, cols), BF)

    def back(t, carry):
        j = doms - 1 - t
        wbuf[j] = (swept[j] + dot(maps[j, 2], wbuf[j + 1])).astype(BF)
        return carry

    lax.fori_loop(0, doms - 1, back, 0, unroll=True)
    inc = ebuf[d]
    outgoing = wbuf[d + 1]
    vw = (dot(wc_h, inc) + dot(wc_l, inc)).astype(BF)
    ve = (dot(ec_h, outgoing) + dot(ec_l, outgoing)).astype(BF)
    sol[z] = (init[...] + dot(gsel[...], jnp.concatenate([vw, ve], axis=0))).astype(BF)
    chunks = o_r.shape[1]
    span = rows // chunks

    def passing(block, c, way):
        ref = sol.at[block, pl.ds(c * span, span), :]
        return pltpu.make_async_remote_copy(
            src_ref=ref, dst_ref=ref, send_sem=o_s.at[way, block, c], recv_sem=o_r.at[block, c],
            device_id={"grp": z + 1 - 2 * way}, device_id_type=MESH)

    def add_picked(block):
        c0 = pl.multiple_of(block * rows, rows)
        return dot(pt[:, pl.ds(c0, rows)], sol[block])

    can = (z < n - 1, z > 0)

    def have(s, way):
        return z >= s if way == 0 else z + s < n

    for s in range(n):
        for c in range(chunks):
            for way in range(2):
                block = z - s if way == 0 else z + s
                if s:
                    @pl.when(have(s, way))
                    def _():
                        passing(block, c, way).wait_recv()

                @pl.when(jnp.logical_and(have(s, way), can[way]))
                def _():
                    passing(block, c, way).start()
        if s == 0:
            picked[...] = add_picked(z)
            continue
        for way in range(2):
            block = z - s if way == 0 else z + s

            @pl.when(have(s, way))
            def _():
                picked[...] += add_picked(block)

    for s in range(n - 1):
        for c in range(chunks):
            for way in range(2):
                block = z - s if way == 0 else z + s

                @pl.when(jnp.logical_and(have(s, way), can[way]))
                def _():
                    passing(block, c, way).wait_send()

    out_ref[...] = (dot(lmt[...], picked[...].astype(BF)) + ll_ref[...].astype(F32)).astype(BF)


def solution(mesh):
    n, doms = mesh.shape["grp"], mesh.shape["dom"]

    def on_device(leaf_load, leaf_map, group_map, node_index, west_coupling, east_coupling):
        nodes, cols = leaf_load.shape[2:]
        rows, interface = group_map.shape[1:]
        face = west_coupling.shape[1]
        fr = rows // (interface // face)
        vm = pl.BlockSpec(memory_space=pltpu.VMEM)
        dma = pltpu.SemaphoreType.DMA
        out = pl.pallas_call(
            functools.partial(kernel, n, doms),
            out_shape=jax.ShapeDtypeStruct((nodes, cols), BF),
            in_specs=[vm, vm, pl.BlockSpec(memory_space=pl.ANY), vm, vm, vm],
            out_specs=vm,
            scratch_shapes=[
                pltpu.VMEM((rows, interface), BF),
                pltpu.VMEM((n, nodes, cols), BF),
                pltpu.VMEM((n, nodes // 128, 128), jnp.int32),
                pltpu.VMEM((interface, cols), F32),
                pltpu.VMEM((interface, cols), BF),
                pltpu.VMEM((interface // 2, face), BF),
                pltpu.VMEM((2 * fr, interface), BF),
                pltpu.VMEM((rows, 2 * face), BF),
                pltpu.VMEM((doms, 3, face, face), BF),
                pltpu.VMEM((doms, 2, face, cols), BF),
                pltpu.VMEM((doms + 1, face, cols), BF),
                pltpu.VMEM((doms + 1, face, cols), BF),
                pltpu.VMEM((doms, face, cols), F32),
                pltpu.VMEM((rows, cols), F32),
                pltpu.VMEM((n, rows, cols), BF),
                pltpu.VMEM((nodes, interface), BF),
                pltpu.VMEM((nodes, nodes), BF),
                pltpu.VMEM((nodes, cols), F32),
                pltpu.VMEM((interface, nodes), BF),
                dma, dma((n,)), dma((n,)), dma((n,)), dma((n,)), dma((n,)), dma((n,)),
                dma((n,)), dma((n,)), dma((2, n, 4)), dma((n, 4)),
                dma((3, doms)), dma((3, doms)), dma((2, doms)), dma((2, doms)),
            ],
            compiler_params=pltpu.CompilerParams(
                collective_id=0, has_side_effects=True, vmem_limit_bytes=60 * 1024 * 1024
            ),
            cost_estimate=pl.CostEstimate(flops=10**10, bytes_accessed=11 * 10**6, transcendentals=0),
        )(
            leaf_map[0, 0], leaf_load[0, 0], group_map[0], node_index.reshape(nodes // 128, 128),
            west_coupling[0], east_coupling[0],
        )
        return out[None, None]

    return jax.shard_map(
        on_device,
        mesh=mesh,
        in_specs=(
            P("dom", "grp", None, None),
            P("dom", "grp", None, None),
            P("dom", "grp", None),
            P("dom", "grp", None),
            P("dom", None, None),
            P("dom", None, None),
        ),
        out_specs=P("dom", "grp", None, None),
        check_vma=False,
    )
```

```python
import functools

import jax
import jax.numpy as jnp
from jax import lax
from jax.experimental import pallas as pl
from jax.experimental.pallas import tpu as pltpu
from jax.sharding import PartitionSpec as P

MESH = pl.DeviceIdType.MESH
BF = jnp.bfloat16
F32 = jnp.float32


def dot(a, b):
    return jnp.dot(a, b, preferred_element_type=F32)


def flip(d, mask):
    out = d
    bit = 1
    while bit <= mask:
        if mask & bit:
            out = out + (1 - 2 * (lax.div(d, bit) % 2)) * bit
        bit *= 2
    return out


def subsets(bits):
    found = [0]
    for bit in bits:
        found += [m | bit for m in found]
    return found


def kernel(
    n, doms,
    lm_ref, ll_ref, g_hbm, idx_ref, wc_ref, ec_ref, out_ref,
    g, contrib, idx_all, loads, loads_b, sel, gface, gsel, maps, faces, ebuf, wbuf, swept, init, sol, pt, lmt, picked, plast,
    g_sem, i_s, i_r, c_s, c_r, m_s, m_r, f_s, f_r, o_s, o_r, ms, mr, fs, fr_,
):
    z = lax.axis_index("grp")
    d = lax.axis_index("dom")
    rows, interface = g.shape
    nodes, cols = ll_ref.shape
    face = wc_ref.shape[0]
    stride = interface // face
    fr = rows // stride
    bits = []
    while (1 << len(bits)) < doms:
        bits.append(1 << len(bits))
    tile = 512

    load_g = pltpu.make_async_copy(g_hbm, g, g_sem)
    load_g.start()
    barrier = pltpu.get_barrier_semaphore()
    for o in range(1, n):
        pl.semaphore_signal(barrier, inc=1, device_id={"grp": (z + o) % n}, device_id_type=MESH)
    for bit in bits:
        pl.semaphore_signal(barrier, inc=1, device_id={"dom": flip(d, bit)}, device_id_type=MESH)

    contrib[z] = dot(lm_ref[...], ll_ref[...]).astype(BF)
    idx_all[z] = idx_ref[...]
    pl.semaphore_wait(barrier, n - 1 + len(bits))

    def to_group(ref, ss, rs):
        made = []
        for o in range(1, n):
            made.append(pltpu.make_async_remote_copy(
                src_ref=ref, dst_ref=ref, send_sem=ss.at[o], recv_sem=rs.at[o],
                device_id={"grp": (z + o) % n}, device_id_type=MESH))
        return made

    def start(copies):
        for c in copies:
            c.start()

    sent = []

    def wait(copies):
        for c in copies:
            c.wait_recv()
        sent.extend(copies)

    i_copies = to_group(idx_all.at[z], i_s, i_r)
    c_copies = to_group(contrib.at[z], c_s, c_r)
    start(i_copies)

    half = interface // 2
    hf = face // 2
    a = lax.broadcasted_iota(jnp.int32, (half, face), 0)
    b = lax.broadcasted_iota(jnp.int32, (half, face), 1)
    want = jnp.where(b < hf, b * stride, (b - hf) * stride + 1)
    sel[...] = jnp.where(a == want, 1.0, 0.0).astype(BF)
    a = lax.broadcasted_iota(jnp.int32, (2 * fr, rows), 0)
    b = lax.broadcasted_iota(jnp.int32, (2 * fr, rows), 1)
    want = jnp.where(a < fr, a * stride, (a - fr) * stride + 1)
    pick_rows = jnp.where(b == want, 1.0, 0.0).astype(BF)

    load_g.wait()
    @pl.loop(0, interface // tile)
    def _(i):
        c0 = pl.multiple_of(i * tile, tile)
        gface[:, pl.ds(c0, tile)] = dot(pick_rows, g[:, pl.ds(c0, tile)]).astype(BF)

    got = [dot(gface[:, c * half:(c + 1) * half], sel[...]).astype(BF) for c in range(2)]
    ff = jnp.concatenate([got[0][:, :hf], got[1][:, :hf], got[0][:, hf:], got[1][:, hf:]], axis=1)

    def split(x):
        high = x.astype(BF)
        return high, (x - high.astype(F32)).astype(BF)

    wc_h, wc_l = split(wc_ref[...])
    ec_h, ec_l = split(ec_ref[...])
    forward = dot(ff[:, :face], wc_h) + dot(ff[:, :face], wc_l)
    backward = dot(ff[:fr, face:], ec_h) + dot(ff[:fr, face:], ec_l)
    z0 = pl.multiple_of(z * fr, fr)
    maps[d, 0, pl.ds(z0, fr), :] = forward[:fr].astype(BF)
    maps[d, 1, pl.ds(z0, fr), :] = forward[fr:].astype(BF)
    maps[d, 2, pl.ds(z0, fr), :] = backward.astype(BF)
    m_copies = to_group(maps.at[d, :, pl.ds(z0, fr), :], m_s, m_r)
    start(m_copies)

    start(c_copies)

    step = min(256, rows)

    @pl.loop(0, rows // step)
    def _(i):
        r0 = pl.multiple_of(i * step, step)
        for c in range(2):
            got = dot(g[pl.ds(r0, step), c * half:(c + 1) * half], sel[...]).astype(BF)
            gsel[pl.ds(r0, step), c * hf:(c + 1) * hf] = got[:, :hf]
            gsel[pl.ds(r0, step), face + c * hf:face + (c + 1) * hf] = got[:, hf:]

    def one_hot(block, r0):
        place = lax.broadcasted_iota(jnp.int32, (tile, 128), 0) + r0
        return jnp.concatenate([
            jnp.where(place == idx_all[block, pl.ds(r, 1), :], 1.0, 0.0).astype(BF)
            for r in range(nodes // 128)], axis=1)

    upper = 2 * z < n
    near = jnp.where(upper, z, n - 1 - z)

    def arrival(t):
        far = jnp.where(upper, z + (t - near + 1), z - (t - near + 1))
        return jnp.where(t < 2 * near, z + (t // 2 + 1) * (1 - t % 2 * 2), far)

    def take(block):
        o = (z - block + n) % n
        pltpu.make_async_remote_copy(
            src_ref=contrib.at[block], dst_ref=contrib.at[block], send_sem=c_s.at[o], recv_sem=c_r.at[o],
            device_id={"grp": block}, device_id_type=MESH).wait_recv()

    def add_loads(block, first):
        @pl.loop(0, interface // tile)
        def _(i):
            r0 = pl.multiple_of(i * tile, tile)
            part = dot(one_hot(block, r0), contrib[block])
            if first:
                loads[pl.ds(r0, tile), :] = part
            else:
                loads[pl.ds(r0, tile), :] += part

    def spread(ref, part, order, ss, rs, pick):
        done, steps = [], []
        for bit in order:
            steps.append([pltpu.make_async_remote_copy(
                src_ref=ref.at[flip(d, m), *pick], dst_ref=ref.at[flip(d, m), *pick],
                send_sem=ss.at[part, m | bit], recv_sem=rs.at[part, m | bit],
                device_id={"dom": flip(d, bit)}, device_id_type=MESH) for m in subsets(done)])
            done.append(bit)
        return steps

    order_a = bits[::-1]
    order_b = order_a if len(bits) < 3 else [order_a[1], order_a[0]] + order_a[2:]
    map_steps = [
        spread(maps, p, (order_a, order_b)[p % 2], ms, mr, (p // 2, pl.ds(p % 2 * hf, hf))) for p in range(6)]
    face_steps = [spread(faces, p, (order_a, order_b)[p], fs, fr_, (p,)) for p in range(2)]

    wait(i_copies)
    add_loads(z, True)
    wait(m_copies)
    for s in map_steps:
        start(s[0])

    turned = jnp.transpose(idx_ref[...])
    for r in range(nodes // 128):
        column = turned[:, r:r + 1]

        @pl.loop(0, interface // tile)
        def _(i):
            c0 = pl.multiple_of(i * tile, tile)
            place = lax.broadcasted_iota(jnp.int32, (128, tile), 1) + c0
            pt[r * 128:(r + 1) * 128, pl.ds(c0, tile)] = jnp.where(place == column, 1.0, 0.0).astype(BF)

    lmt[...] = jnp.transpose(lm_ref[...])

    if len(bits) > 1:
        for s in map_steps:
            wait(s[0])
            start(s[1])

    last = arrival(n - 2)
    gp = jnp.zeros((2 * fr, nodes), F32)

    def prepare(i, gp):
        r0 = pl.multiple_of(i * tile, tile)
        hot = one_hot(last, r0)
        plast[pl.ds(r0, tile), :] = hot
        return gp + dot(gface[:, pl.ds(r0, tile)], hot)

    gp = lax.fori_loop(0, interface // tile, prepare, gp).astype(BF)

    for t in range(n - 2):
        block = arrival(t)
        take(block)
        add_loads(block, False)
    for k in range(2, len(bits)):
        for s in map_steps:
            wait(s[k - 1])
            start(s[k])

    here = dot(gface[...], loads[...].astype(BF))
    take(last)
    sent.extend(c_copies)
    here = (here + dot(gp, contrib[last])).astype(BF)
    faces[d, 0, pl.ds(z0, fr), :] = here[:fr]
    faces[d, 1, pl.ds(z0, fr), :] = here[fr:]
    f_copies = to_group(faces.at[d, :, pl.ds(z0, fr), :], f_s, f_r)
    start(f_copies)

    @pl.loop(0, interface // tile)
    def _(i):
        r0 = pl.multiple_of(i * tile, tile)
        loads_b[pl.ds(r0, tile), :] = (loads[pl.ds(r0, tile), :] + dot(plast[pl.ds(r0, tile), :], contrib[last])).astype(BF)

    wait(f_copies)
    for s in face_steps:
        start(s[0])

    @pl.loop(0, rows // step)
    def _(i):
        r0 = pl.multiple_of(i * step, step)
        init[pl.ds(r0, step), :] = dot(g[pl.ds(r0, step), :], loads_b[...])

    for k in range(1, len(bits)):
        for s in face_steps:
            wait(s[k - 1])
            start(s[k])
    for s in map_steps:
        wait(s[-1])
    for s in face_steps:
        wait(s[-1])

    ebuf[0] = jnp.zeros((face, cols), BF)
    ebuf[1] = faces[0, 1]

    def ahead(j, carry):
        both = maps[j, pl.ds(0, 2)].reshape(2 * face, face)
        got = dot(both, ebuf[j])
        swept[j] = got[:face] + faces[j, 0].astype(F32)
        ebuf[j + 1] = (got[face:] + faces[j, 1].astype(F32)).astype(BF)
        return carry

    lax.fori_loop(1, doms, ahead, 0, unroll=True)
    wbuf[doms] = jnp.zeros((face, cols), BF)

    def back(t, carry):
        j = doms - 1 - t
        wbuf[j] = (swept[j] + dot(maps[j, 2], wbuf[j + 1])).astype(BF)
        return carry

    lax.fori_loop(0, doms - 1, back, 0, unroll=True)
    inc = ebuf[d]
    outgoing = wbuf[d + 1]
    vw = (dot(wc_h, inc) + dot(wc_l, inc)).astype(BF)
    ve = (dot(ec_h, outgoing) + dot(ec_l, outgoing)).astype(BF)
    sol[z] = (init[...] + dot(gsel[...], jnp.concatenate([vw, ve], axis=0))).astype(BF)
    chunks = o_r.shape[1]
    span = rows // chunks

    def passing(block, c, way):
        ref = sol.at[block, pl.ds(c * span, span), :]
        return pltpu.make_async_remote_copy(
            src_ref=ref, dst_ref=ref, send_sem=o_s.at[way, block, c], recv_sem=o_r.at[block, c],
            device_id={"grp": z + 1 - 2 * way}, device_id_type=MESH)

    def add_picked(block):
        c0 = pl.multiple_of(block * rows, rows)
        return dot(pt[:, pl.ds(c0, rows)], sol[block])

    can = (z < n - 1, z > 0)

    def have(s, way):
        return z >= s if way == 0 else z + s < n

    for s in range(n):
        for c in range(chunks):
            for way in range(2):
                block = z - s if way == 0 else z + s
                if s:
                    @pl.when(have(s, way))
                    def _():
                        passing(block, c, way).wait_recv()

                @pl.when(jnp.logical_and(have(s, way), can[way]))
                def _():
                    passing(block, c, way).start()
        if s == 0:
            picked[...] = add_picked(z)
            continue
        for way in range(2):
            block = z - s if way == 0 else z + s

            @pl.when(have(s, way))
            def _():
                picked[...] += add_picked(block)

    for c in sent:
        c.wait_send()
    for s in range(n - 1):
        for c in range(chunks):
            for way in range(2):
                block = z - s if way == 0 else z + s

                @pl.when(jnp.logical_and(have(s, way), can[way]))
                def _():
                    passing(block, c, way).wait_send()

    out_ref[...] = (dot(lmt[...], picked[...].astype(BF)) + ll_ref[...].astype(F32)).astype(BF)


def solution(mesh):
    n, doms = mesh.shape["grp"], mesh.shape["dom"]

    def on_device(leaf_load, leaf_map, group_map, node_index, west_coupling, east_coupling):
        nodes, cols = leaf_load.shape[2:]
        rows, interface = group_map.shape[1:]
        face = west_coupling.shape[1]
        fr = rows // (interface // face)
        vm = pl.BlockSpec(memory_space=pltpu.VMEM)
        dma = pltpu.SemaphoreType.DMA
        out = pl.pallas_call(
            functools.partial(kernel, n, doms),
            out_shape=jax.ShapeDtypeStruct((nodes, cols), BF),
            in_specs=[vm, vm, pl.BlockSpec(memory_space=pl.ANY), vm, vm, vm],
            out_specs=vm,
            scratch_shapes=[
                pltpu.VMEM((rows, interface), BF),
                pltpu.VMEM((n, nodes, cols), BF),
                pltpu.VMEM((n, nodes // 128, 128), jnp.int32),
                pltpu.VMEM((interface, cols), F32),
                pltpu.VMEM((interface, cols), BF),
                pltpu.VMEM((interface // 2, face), BF),
                pltpu.VMEM((2 * fr, interface), BF),
                pltpu.VMEM((rows, 2 * face), BF),
                pltpu.VMEM((doms, 3, face, face), BF),
                pltpu.VMEM((doms, 2, face, cols), BF),
                pltpu.VMEM((doms + 1, face, cols), BF),
                pltpu.VMEM((doms + 1, face, cols), BF),
                pltpu.VMEM((doms, face, cols), F32),
                pltpu.VMEM((rows, cols), F32),
                pltpu.VMEM((n, rows, cols), BF),
                pltpu.VMEM((nodes, interface), BF),
                pltpu.VMEM((nodes, nodes), BF),
                pltpu.VMEM((nodes, cols), F32),
                pltpu.VMEM((interface, nodes), BF),
                dma, dma((n,)), dma((n,)), dma((n,)), dma((n,)), dma((n,)), dma((n,)),
                dma((n,)), dma((n,)), dma((2, n, 4)), dma((n, 4)),
                dma((6, doms)), dma((6, doms)), dma((2, doms)), dma((2, doms)),
            ],
            compiler_params=pltpu.CompilerParams(
                collective_id=0, has_side_effects=True, vmem_limit_bytes=60 * 1024 * 1024
            ),
            cost_estimate=pl.CostEstimate(flops=10**10, bytes_accessed=11 * 10**6, transcendentals=0),
        )(
            leaf_map[0, 0], leaf_load[0, 0], group_map[0], node_index.reshape(nodes // 128, 128),
            west_coupling[0], east_coupling[0],
        )
        return out[None, None]

    return jax.shard_map(
        on_device,
        mesh=mesh,
        in_specs=(
            P("dom", "grp", None, None),
            P("dom", "grp", None, None),
            P("dom", "grp", None),
            P("dom", "grp", None),
            P("dom", None, None),
            P("dom", None, None),
        ),
        out_specs=P("dom", "grp", None, None),
        check_vma=False,
    )
```

```python
import functools

import jax
import jax.numpy as jnp
from jax import lax
from jax.experimental import pallas as pl
from jax.experimental.pallas import tpu as pltpu
from jax.sharding import PartitionSpec as P

MESH = pl.DeviceIdType.MESH
BF = jnp.bfloat16
F32 = jnp.float32


def dot(a, b):
    return jnp.dot(a, b, preferred_element_type=F32)


def flip(d, mask):
    out = d
    bit = 1
    while bit <= mask:
        if mask & bit:
            out = out + (1 - 2 * (lax.div(d, bit) % 2)) * bit
        bit *= 2
    return out


def subsets(bits):
    found = [0]
    for bit in bits:
        found += [m | bit for m in found]
    return found


def kernel(
    n, doms,
    lm_ref, ll_ref, g_hbm, idx_ref, wc_ref, ec_ref, out_ref,
    g, contrib, idx_all, loads, loads_b, sel, gface, gsel, maps, faces, ebuf, wbuf, swept, init, sol, pt, lmt, picked, plast,
    g_sem, i_s, i_r, c_s, c_r, m_s, m_r, f_s, f_r, o_s, o_r, ms, mr, fs, fr_,
):
    z = lax.axis_index("grp")
    d = lax.axis_index("dom")
    rows, interface = g.shape
    nodes, cols = ll_ref.shape
    face = wc_ref.shape[0]
    stride = interface // face
    fr = rows // stride
    bits = []
    while (1 << len(bits)) < doms:
        bits.append(1 << len(bits))
    tile = 512

    load_g = pltpu.make_async_copy(g_hbm, g, g_sem)
    load_g.start()
    barrier = pltpu.get_barrier_semaphore()
    for o in range(1, n):
        pl.semaphore_signal(barrier, inc=1, device_id={"grp": (z + o) % n}, device_id_type=MESH)
    for bit in bits:
        pl.semaphore_signal(barrier, inc=1, device_id={"dom": flip(d, bit)}, device_id_type=MESH)

    contrib[z] = dot(lm_ref[...], ll_ref[...]).astype(BF)
    idx_all[z] = idx_ref[...]
    pl.semaphore_wait(barrier, n - 1 + len(bits))

    def to_group(ref, ss, rs):
        made = []
        for o in range(1, n):
            made.append(pltpu.make_async_remote_copy(
                src_ref=ref, dst_ref=ref, send_sem=ss.at[o], recv_sem=rs.at[o],
                device_id={"grp": (z + o) % n}, device_id_type=MESH))
        return made

    def start(copies):
        for c in copies:
            c.start()

    sent = []

    def wait(copies):
        for c in copies:
            c.wait_recv()
        sent.extend(copies)

    i_copies = to_group(idx_all.at[z], i_s, i_r)
    c_copies = to_group(contrib.at[z], c_s, c_r)
    start(i_copies)

    half = interface // 2
    hf = face // 2
    a = lax.broadcasted_iota(jnp.int32, (half, face), 0)
    b = lax.broadcasted_iota(jnp.int32, (half, face), 1)
    want = jnp.where(b < hf, b * stride, (b - hf) * stride + 1)
    sel[...] = jnp.where(a == want, 1.0, 0.0).astype(BF)
    a = lax.broadcasted_iota(jnp.int32, (2 * fr, rows), 0)
    b = lax.broadcasted_iota(jnp.int32, (2 * fr, rows), 1)
    want = jnp.where(a < fr, a * stride, (a - fr) * stride + 1)
    pick_rows = jnp.where(b == want, 1.0, 0.0).astype(BF)

    load_g.wait()
    @pl.loop(0, interface // tile)
    def _(i):
        c0 = pl.multiple_of(i * tile, tile)
        gface[:, pl.ds(c0, tile)] = dot(pick_rows, g[:, pl.ds(c0, tile)]).astype(BF)

    got = [dot(gface[:, c * half:(c + 1) * half], sel[...]).astype(BF) for c in range(2)]
    ff = jnp.concatenate([got[0][:, :hf], got[1][:, :hf], got[0][:, hf:], got[1][:, hf:]], axis=1)

    def split(x):
        high = x.astype(BF)
        return high, (x - high.astype(F32)).astype(BF)

    wc_h, wc_l = split(wc_ref[...])
    ec_h, ec_l = split(ec_ref[...])
    forward = dot(ff[:, :face], wc_h) + dot(ff[:, :face], wc_l)
    backward = dot(ff[:fr, face:], ec_h) + dot(ff[:fr, face:], ec_l)
    z0 = pl.multiple_of(z * fr, fr)
    maps[d, 0, pl.ds(z0, fr), :] = forward[:fr].astype(BF)
    maps[d, 1, pl.ds(z0, fr), :] = forward[fr:].astype(BF)
    maps[d, 2, pl.ds(z0, fr), :] = backward.astype(BF)
    m_copies = to_group(maps.at[d, :, pl.ds(z0, fr), :], m_s, m_r)
    start(m_copies)

    start(c_copies)

    place = lax.broadcasted_iota(jnp.int32, (tile, 128), 0).astype(jnp.int16)

    def one_hot(block, r0):
        made = []
        for r in range(nodes // 128):
            row = jnp.broadcast_to(idx_all[block, pl.ds(r, 1), :] - r0, (16, 128)).astype(jnp.int16)
            row = jnp.concatenate([row] * (tile // 16), axis=0)
            made.append(jnp.where(place == row, jnp.ones((), BF), jnp.zeros((), BF)))
        return jnp.concatenate(made, axis=1)

    upper = 2 * z < n
    near = jnp.where(upper, z, n - 1 - z)

    def arrival(t):
        far = jnp.where(upper, z + (t - near + 1), z - (t - near + 1))
        return jnp.where(t < 2 * near, z + (t // 2 + 1) * (1 - t % 2 * 2), far)

    def take(block):
        o = (z - block + n) % n
        pltpu.make_async_remote_copy(
            src_ref=contrib.at[block], dst_ref=contrib.at[block], send_sem=c_s.at[o], recv_sem=c_r.at[o],
            device_id={"grp": block}, device_id_type=MESH).wait_recv()

    def add_loads(block, first):
        @pl.loop(0, interface // tile)
        def _(i):
            r0 = pl.multiple_of(i * tile, tile)
            part = dot(one_hot(block, r0), contrib[block])
            if first:
                loads[pl.ds(r0, tile), :] = part
            else:
                loads[pl.ds(r0, tile), :] += part

    def spread(ref, part, order, ss, rs, pick):
        done, steps = [], []
        for bit in order:
            steps.append([pltpu.make_async_remote_copy(
                src_ref=ref.at[flip(d, m), *pick], dst_ref=ref.at[flip(d, m), *pick],
                send_sem=ss.at[part, m | bit], recv_sem=rs.at[part, m | bit],
                device_id={"dom": flip(d, bit)}, device_id_type=MESH) for m in subsets(done)])
            done.append(bit)
        return steps

    order_a = bits[::-1]
    order_b = order_a if len(bits) < 3 else [order_a[1], order_a[0]] + order_a[2:]
    map_steps = [
        spread(maps, p, (order_a, order_b)[p % 2], ms, mr, (p // 2, pl.ds(p % 2 * hf, hf))) for p in range(6)]
    face_steps = [spread(faces, p, (order_a, order_b)[p], fs, fr_, (p,)) for p in range(2)]

    wait(i_copies)
    add_loads(z, True)
    wait(m_copies)
    for s in map_steps:
        start(s[0])

    last = arrival(n - 2)
    gp = jnp.zeros((2 * fr, nodes), F32)

    def prepare(i, gp):
        r0 = pl.multiple_of(i * tile, tile)
        hot = one_hot(last, r0)
        plast[pl.ds(r0, tile), :] = hot
        return gp + dot(gface[:, pl.ds(r0, tile)], hot)

    gp = lax.fori_loop(0, interface // tile, prepare, gp).astype(BF)

    if len(bits) > 1:
        for s in map_steps:
            wait(s[0])
            start(s[1])

    for t in range(n - 2):
        block = arrival(t)
        take(block)
        add_loads(block, False)
    for k in range(2, len(bits)):
        for s in map_steps:
            wait(s[k - 1])
            start(s[k])

    here = dot(gface[...], loads[...].astype(BF))
    take(last)
    sent.extend(c_copies)
    here = (here + dot(gp, contrib[last])).astype(BF)
    faces[d, 0, pl.ds(z0, fr), :] = here[:fr]
    faces[d, 1, pl.ds(z0, fr), :] = here[fr:]
    f_copies = to_group(faces.at[d, :, pl.ds(z0, fr), :], f_s, f_r)
    start(f_copies)

    @pl.loop(0, interface // tile)
    def _(i):
        r0 = pl.multiple_of(i * tile, tile)
        loads_b[pl.ds(r0, tile), :] = (loads[pl.ds(r0, tile), :] + dot(plast[pl.ds(r0, tile), :], contrib[last])).astype(BF)

    wait(f_copies)
    for s in face_steps:
        start(s[0])

    step = min(256, rows)

    def take_columns():
        @pl.loop(0, rows // step)
        def _(i):
            r0 = pl.multiple_of(i * step, step)
            for c in range(2):
                got = dot(g[pl.ds(r0, step), c * half:(c + 1) * half], sel[...]).astype(BF)
                gsel[pl.ds(r0, step), c * hf:(c + 1) * hf] = got[:, :hf]
                gsel[pl.ds(r0, step), face + c * hf:face + (c + 1) * hf] = got[:, hf:]

    def start_rows():
        @pl.loop(0, rows // step)
        def _(i):
            r0 = pl.multiple_of(i * step, step)
            init[pl.ds(r0, step), :] = dot(g[pl.ds(r0, step), :], loads_b[...])

    def turn_map():
        lmt[...] = jnp.transpose(lm_ref[...])

    beside = [take_columns, start_rows, turn_map]
    for k in range(1, len(bits)):
        if beside:
            beside.pop(0)()
        for s in face_steps:
            wait(s[k - 1])
            start(s[k])
    for work in beside:
        work()
    for s in map_steps:
        wait(s[-1])
    for s in face_steps:
        wait(s[-1])

    ebuf[0] = jnp.zeros((face, cols), BF)
    east = faces[0, 1]
    ebuf[1] = east
    for j in range(1, doms):
        swept[j] = dot(maps[j, 0], east) + faces[j, 0].astype(F32)
        if j < doms - 1:
            east = (dot(maps[j, 1], east) + faces[j, 1].astype(F32)).astype(BF)
            ebuf[j + 1] = east
    wbuf[doms] = jnp.zeros((face, cols), BF)
    west = swept[doms - 1].astype(BF)
    wbuf[doms - 1] = west
    for j in range(doms - 2, 0, -1):
        west = (swept[j] + dot(maps[j, 2], west)).astype(BF)
        wbuf[j] = west
    inc = ebuf[d]
    outgoing = wbuf[d + 1]
    vw = (dot(wc_h, inc) + dot(wc_l, inc)).astype(BF)
    ve = (dot(ec_h, outgoing) + dot(ec_l, outgoing)).astype(BF)
    sol[z] = (init[...] + dot(gsel[...], jnp.concatenate([vw, ve], axis=0))).astype(BF)
    chunks = o_r.shape[1]
    span = rows // chunks

    def passing(block, c, way):
        ref = sol.at[block, pl.ds(c * span, span), :]
        return pltpu.make_async_remote_copy(
            src_ref=ref, dst_ref=ref, send_sem=o_s.at[way, block, c], recv_sem=o_r.at[block, c],
            device_id={"grp": z + 1 - 2 * way}, device_id_type=MESH)

    def turn_index():
        turned = jnp.transpose(idx_ref[...])
        for r in range(nodes // 128):
            column = turned[:, r:r + 1]

            @pl.loop(0, interface // tile)
            def _(i):
                c0 = pl.multiple_of(i * tile, tile)
                place = lax.broadcasted_iota(jnp.int32, (128, tile), 1) + c0
                pt[r * 128:(r + 1) * 128, pl.ds(c0, tile)] = jnp.where(place == column, 1.0, 0.0).astype(BF)

    def add_picked(block):
        c0 = pl.multiple_of(block * rows, rows)
        return dot(pt[:, pl.ds(c0, rows)], sol[block])

    can = (z < n - 1, z > 0)

    def have(s, way):
        return z >= s if way == 0 else z + s < n

    for s in range(n):
        for c in range(chunks):
            for way in range(2):
                block = z - s if way == 0 else z + s
                if s:
                    @pl.when(have(s, way))
                    def _():
                        passing(block, c, way).wait_recv()

                @pl.when(jnp.logical_and(have(s, way), can[way]))
                def _():
                    passing(block, c, way).start()
        if s == 0:
            turn_index()
            picked[...] = add_picked(z)
            continue
        for way in range(2):
            block = z - s if way == 0 else z + s

            @pl.when(have(s, way))
            def _():
                picked[...] += add_picked(block)

    for c in sent:
        c.wait_send()
    for s in range(n - 1):
        for c in range(chunks):
            for way in range(2):
                block = z - s if way == 0 else z + s

                @pl.when(jnp.logical_and(have(s, way), can[way]))
                def _():
                    passing(block, c, way).wait_send()

    out_ref[...] = (dot(lmt[...], picked[...].astype(BF)) + ll_ref[...].astype(F32)).astype(BF)


def solution(mesh):
    n, doms = mesh.shape["grp"], mesh.shape["dom"]

    def on_device(leaf_load, leaf_map, group_map, node_index, west_coupling, east_coupling):
        nodes, cols = leaf_load.shape[2:]
        rows, interface = group_map.shape[1:]
        face = west_coupling.shape[1]
        fr = rows // (interface // face)
        vm = pl.BlockSpec(memory_space=pltpu.VMEM)
        dma = pltpu.SemaphoreType.DMA
        out = pl.pallas_call(
            functools.partial(kernel, n, doms),
            out_shape=jax.ShapeDtypeStruct((nodes, cols), BF),
            in_specs=[vm, vm, pl.BlockSpec(memory_space=pl.ANY), vm, vm, vm],
            out_specs=vm,
            scratch_shapes=[
                pltpu.VMEM((rows, interface), BF),
                pltpu.VMEM((n, nodes, cols), BF),
                pltpu.VMEM((n, nodes // 128, 128), jnp.int32),
                pltpu.VMEM((interface, cols), F32),
                pltpu.VMEM((interface, cols), BF),
                pltpu.VMEM((interface // 2, face), BF),
                pltpu.VMEM((2 * fr, interface), BF),
                pltpu.VMEM((rows, 2 * face), BF),
                pltpu.VMEM((doms, 3, face, face), BF),
                pltpu.VMEM((doms, 2, face, cols), BF),
                pltpu.VMEM((doms + 1, face, cols), BF),
                pltpu.VMEM((doms + 1, face, cols), BF),
                pltpu.VMEM((doms, face, cols), F32),
                pltpu.VMEM((rows, cols), F32),
                pltpu.VMEM((n, rows, cols), BF),
                pltpu.VMEM((nodes, interface), BF),
                pltpu.VMEM((nodes, nodes), BF),
                pltpu.VMEM((nodes, cols), F32),
                pltpu.VMEM((interface, nodes), BF),
                dma, dma((n,)), dma((n,)), dma((n,)), dma((n,)), dma((n,)), dma((n,)),
                dma((n,)), dma((n,)), dma((2, n, 4)), dma((n, 4)),
                dma((6, doms)), dma((6, doms)), dma((2, doms)), dma((2, doms)),
            ],
            compiler_params=pltpu.CompilerParams(
                collective_id=0, has_side_effects=True, vmem_limit_bytes=60 * 1024 * 1024
            ),
            cost_estimate=pl.CostEstimate(flops=10**10, bytes_accessed=11 * 10**6, transcendentals=0),
        )(
            leaf_map[0, 0], leaf_load[0, 0], group_map[0], node_index.reshape(nodes // 128, 128),
            west_coupling[0], east_coupling[0],
        )
        return out[None, None]

    return jax.shard_map(
        on_device,
        mesh=mesh,
        in_specs=(
            P("dom", "grp", None, None),
            P("dom", "grp", None, None),
            P("dom", "grp", None),
            P("dom", "grp", None),
            P("dom", None, None),
            P("dom", None, None),
        ),
        out_specs=P("dom", "grp", None, None),
        check_vma=False,
    )
```

```python
import functools

import jax
import jax.numpy as jnp
from jax import lax
from jax.experimental import pallas as pl
from jax.experimental.pallas import tpu as pltpu
from jax.sharding import PartitionSpec as P

MESH = pl.DeviceIdType.MESH
BF = jnp.bfloat16
F32 = jnp.float32


def dot(a, b):
    return jnp.dot(a, b, preferred_element_type=F32)


def flip(d, mask):
    out = d
    bit = 1
    while bit <= mask:
        if mask & bit:
            out = out + (1 - 2 * (lax.div(d, bit) % 2)) * bit
        bit *= 2
    return out


def subsets(bits):
    found = [0]
    for bit in bits:
        found += [m | bit for m in found]
    return found


def kernel(
    n, doms,
    lm_ref, ll_ref, g_hbm, idx_ref, wc_ref, ec_ref, out_ref,
    g, contrib, idx_all, loads, loads_b, sel, gface, gsel, maps, faces, ebuf, wbuf, swept, init, sol, pt, lmt, picked, plast,
    g_sem, i_s, i_r, c_s, c_r, m_s, m_r, f_s, f_r, o_s, o_r, ms, mr, fs, fr_,
):
    z = lax.axis_index("grp")
    d = lax.axis_index("dom")
    rows, interface = g.shape
    nodes, cols = ll_ref.shape
    face = wc_ref.shape[0]
    stride = interface // face
    fr = rows // stride
    bits = []
    while (1 << len(bits)) < doms:
        bits.append(1 << len(bits))
    tile = 512

    load_g = pltpu.make_async_copy(g_hbm, g, g_sem)
    load_g.start()
    barrier = pltpu.get_barrier_semaphore()
    for o in range(1, n):
        pl.semaphore_signal(barrier, inc=1, device_id={"grp": (z + o) % n}, device_id_type=MESH)
    for bit in bits:
        pl.semaphore_signal(barrier, inc=1, device_id={"dom": flip(d, bit)}, device_id_type=MESH)

    contrib[z] = dot(lm_ref[...], ll_ref[...]).astype(BF)
    idx_all[z] = idx_ref[...]
    pl.semaphore_wait(barrier, n - 1 + len(bits))

    def to_group(ref, ss, rs):
        made = []
        for o in range(1, n):
            made.append(pltpu.make_async_remote_copy(
                src_ref=ref, dst_ref=ref, send_sem=ss.at[o], recv_sem=rs.at[o],
                device_id={"grp": (z + o) % n}, device_id_type=MESH))
        return made

    def start(copies):
        for c in copies:
            c.start()

    sent = []

    def wait(copies):
        for c in copies:
            c.wait_recv()
        sent.extend(copies)

    can = (z < n - 1, z > 0)

    def have(s, way):
        return z >= s if way == 0 else z + s < n

    def line(buf, ss, rs):
        chunks = rs.shape[1]
        span = buf.shape[1] // chunks

        def passing(block, c, way):
            ref = buf.at[block, pl.ds(c * span, span), :]
            return pltpu.make_async_remote_copy(
                src_ref=ref, dst_ref=ref, send_sem=ss.at[way, block, c], recv_sem=rs.at[block, c],
                device_id={"grp": z + 1 - 2 * way}, device_id_type=MESH)

        def move(s):
            for c in range(chunks):
                for way in range(2):
                    block = z - s if way == 0 else z + s
                    if s:
                        @pl.when(have(s, way))
                        def _():
                            passing(block, c, way).wait_recv()

                    @pl.when(jnp.logical_and(have(s, way), can[way]))
                    def _():
                        passing(block, c, way).start()

        def end():
            for s in range(n - 1):
                for c in range(chunks):
                    for way in range(2):
                        block = z - s if way == 0 else z + s

                        @pl.when(jnp.logical_and(have(s, way), can[way]))
                        def _():
                            passing(block, c, way).wait_send()

        return move, end

    move_contrib, end_contrib = line(contrib, c_s, c_r)
    move_sol, end_sol = line(sol, o_s, o_r)
    i_copies = to_group(idx_all.at[z], i_s, i_r)
    start(i_copies)

    half = interface // 2
    hf = face // 2
    a = lax.broadcasted_iota(jnp.int32, (half, face), 0)
    b = lax.broadcasted_iota(jnp.int32, (half, face), 1)
    want = jnp.where(b < hf, b * stride, (b - hf) * stride + 1)
    sel[...] = jnp.where(a == want, 1.0, 0.0).astype(BF)
    a = lax.broadcasted_iota(jnp.int32, (2 * fr, rows), 0)
    b = lax.broadcasted_iota(jnp.int32, (2 * fr, rows), 1)
    want = jnp.where(a < fr, a * stride, (a - fr) * stride + 1)
    pick_rows = jnp.where(b == want, 1.0, 0.0).astype(BF)

    load_g.wait()
    @pl.loop(0, interface // tile)
    def _(i):
        c0 = pl.multiple_of(i * tile, tile)
        gface[:, pl.ds(c0, tile)] = dot(pick_rows, g[:, pl.ds(c0, tile)]).astype(BF)

    got = [dot(gface[:, c * half:(c + 1) * half], sel[...]).astype(BF) for c in range(2)]
    ff = jnp.concatenate([got[0][:, :hf], got[1][:, :hf], got[0][:, hf:], got[1][:, hf:]], axis=1)

    def split(x):
        high = x.astype(BF)
        return high, (x - high.astype(F32)).astype(BF)

    wc_h, wc_l = split(wc_ref[...])
    ec_h, ec_l = split(ec_ref[...])
    forward = dot(ff[:, :face], wc_h) + dot(ff[:, :face], wc_l)
    backward = dot(ff[:fr, face:], ec_h) + dot(ff[:fr, face:], ec_l)
    z0 = pl.multiple_of(z * fr, fr)
    maps[d, 0, pl.ds(z0, fr), :] = forward[:fr].astype(BF)
    maps[d, 1, pl.ds(z0, fr), :] = forward[fr:].astype(BF)
    maps[d, 2, pl.ds(z0, fr), :] = backward.astype(BF)
    m_copies = to_group(maps.at[d, :, pl.ds(z0, fr), :], m_s, m_r)
    start(m_copies)

    move_contrib(0)

    place = lax.broadcasted_iota(jnp.int32, (tile, 128), 0).astype(jnp.int16)

    def one_hot(block, r0):
        made = []
        for r in range(nodes // 128):
            row = jnp.broadcast_to(idx_all[block, pl.ds(r, 1), :] - r0, (16, 128)).astype(jnp.int16)
            row = jnp.concatenate([row] * (tile // 16), axis=0)
            made.append(jnp.where(place == row, jnp.ones((), BF), jnp.zeros((), BF)))
        return jnp.concatenate(made, axis=1)

    upper = 2 * z < n
    near = jnp.where(upper, z, n - 1 - z)

    def arrival(t):
        far = jnp.where(upper, z + (t - near + 1), z - (t - near + 1))
        return jnp.where(t < 2 * near, z + (t // 2 + 1) * (1 - t % 2 * 2), far)

    def add_loads(block, first):
        @pl.loop(0, interface // tile)
        def _(i):
            r0 = pl.multiple_of(i * tile, tile)
            part = dot(one_hot(block, r0), contrib[block])
            if first:
                loads[pl.ds(r0, tile), :] = part
            else:
                loads[pl.ds(r0, tile), :] += part

    def spread(ref, part, order, ss, rs, pick):
        done, steps = [], []
        for bit in order:
            steps.append([pltpu.make_async_remote_copy(
                src_ref=ref.at[flip(d, m), *pick], dst_ref=ref.at[flip(d, m), *pick],
                send_sem=ss.at[part, m | bit], recv_sem=rs.at[part, m | bit],
                device_id={"dom": flip(d, bit)}, device_id_type=MESH) for m in subsets(done)])
            done.append(bit)
        return steps

    order_a = bits[::-1]
    order_b = order_a if len(bits) < 3 else [order_a[1], order_a[0]] + order_a[2:]
    map_steps = [
        spread(maps, p, (order_a, order_b)[p % 2], ms, mr, (p // 2, pl.ds(p % 2 * hf, hf))) for p in range(6)]
    face_steps = [spread(faces, p, (order_a, order_b)[p], fs, fr_, (p,)) for p in range(2)]

    def turn_index():
        turned = jnp.transpose(idx_ref[...])
        for r in range(nodes // 128):
            column = turned[:, r:r + 1]

            @pl.loop(0, interface // tile)
            def _(i):
                c0 = pl.multiple_of(i * tile, tile)
                place = lax.broadcasted_iota(jnp.int32, (128, tile), 1) + c0
                pt[r * 128:(r + 1) * 128, pl.ds(c0, tile)] = jnp.where(place == column, 1.0, 0.0).astype(BF)

    wait(i_copies)
    add_loads(z, True)
    turn_index()
    wait(m_copies)
    for s in map_steps:
        start(s[0])

    last = arrival(n - 2)
    gp = jnp.zeros((2 * fr, nodes), F32)

    def prepare(i, gp):
        r0 = pl.multiple_of(i * tile, tile)
        hot = one_hot(last, r0)
        plast[pl.ds(r0, tile), :] = hot
        return gp + dot(gface[:, pl.ds(r0, tile)], hot)

    gp = lax.fori_loop(0, interface // tile, prepare, gp).astype(BF)

    if len(bits) > 1:
        for s in map_steps:
            wait(s[0])
            start(s[1])

    for t in range(n - 2):
        move_contrib(t + 1)
        if 1 <= t < len(bits) - 1:
            for s in map_steps:
                wait(s[t])
                start(s[t + 1])
        add_loads(arrival(t), False)
    for k in range(max(n - 1, 2), len(bits)):
        for s in map_steps:
            wait(s[k - 1])
            start(s[k])

    here = dot(gface[...], loads[...].astype(BF))
    move_contrib(n - 1)
    here = (here + dot(gp, contrib[last])).astype(BF)
    faces[d, 0, pl.ds(z0, fr), :] = here[:fr]
    faces[d, 1, pl.ds(z0, fr), :] = here[fr:]
    f_copies = to_group(faces.at[d, :, pl.ds(z0, fr), :], f_s, f_r)
    start(f_copies)

    @pl.loop(0, interface // tile)
    def _(i):
        r0 = pl.multiple_of(i * tile, tile)
        loads_b[pl.ds(r0, tile), :] = (loads[pl.ds(r0, tile), :] + dot(plast[pl.ds(r0, tile), :], contrib[last])).astype(BF)

    wait(f_copies)
    for s in face_steps:
        start(s[0])

    step = min(256, rows)

    def take_columns():
        @pl.loop(0, rows // step)
        def _(i):
            r0 = pl.multiple_of(i * step, step)
            for c in range(2):
                got = dot(g[pl.ds(r0, step), c * half:(c + 1) * half], sel[...]).astype(BF)
                gsel[pl.ds(r0, step), c * hf:(c + 1) * hf] = got[:, :hf]
                gsel[pl.ds(r0, step), face + c * hf:face + (c + 1) * hf] = got[:, hf:]

    def start_rows():
        @pl.loop(0, rows // step)
        def _(i):
            r0 = pl.multiple_of(i * step, step)
            init[pl.ds(r0, step), :] = dot(g[pl.ds(r0, step), :], loads_b[...])

    def turn_map():
        lmt[...] = jnp.transpose(lm_ref[...])

    beside = [take_columns, start_rows, turn_map]
    for k in range(1, len(bits)):
        if beside:
            beside.pop(0)()
        for s in face_steps:
            wait(s[k - 1])
            start(s[k])
    for work in beside:
        work()
    for s in map_steps:
        wait(s[-1])
    for s in face_steps:
        wait(s[-1])

    ebuf[0] = jnp.zeros((face, cols), BF)
    east = faces[0, 1]
    ebuf[1] = east
    for j in range(1, doms):
        swept[j] = dot(maps[j, 0], east) + faces[j, 0].astype(F32)
        if j < doms - 1:
            east = (dot(maps[j, 1], east) + faces[j, 1].astype(F32)).astype(BF)
            ebuf[j + 1] = east
    wbuf[doms] = jnp.zeros((face, cols), BF)
    west = swept[doms - 1].astype(BF)
    wbuf[doms - 1] = west
    for j in range(doms - 2, 0, -1):
        west = (swept[j] + dot(maps[j, 2], west)).astype(BF)
        wbuf[j] = west
    inc = ebuf[d]
    outgoing = wbuf[d + 1]
    vw = (dot(wc_h, inc) + dot(wc_l, inc)).astype(BF)
    ve = (dot(ec_h, outgoing) + dot(ec_l, outgoing)).astype(BF)
    sol[z] = (init[...] + dot(gsel[...], jnp.concatenate([vw, ve], axis=0))).astype(BF)
    def add_picked(block):
        c0 = pl.multiple_of(block * rows, rows)
        return dot(pt[:, pl.ds(c0, rows)], sol[block])

    for s in range(n):
        move_sol(s)
        if s == 0:
            picked[...] = add_picked(z)
            continue
        for way in range(2):
            block = z - s if way == 0 else z + s

            @pl.when(have(s, way))
            def _():
                picked[...] += add_picked(block)

    for c in sent:
        c.wait_send()
    end_contrib()
    end_sol()

    out_ref[...] = (dot(lmt[...], picked[...].astype(BF)) + ll_ref[...].astype(F32)).astype(BF)


def solution(mesh):
    n, doms = mesh.shape["grp"], mesh.shape["dom"]

    def on_device(leaf_load, leaf_map, group_map, node_index, west_coupling, east_coupling):
        nodes, cols = leaf_load.shape[2:]
        rows, interface = group_map.shape[1:]
        face = west_coupling.shape[1]
        fr = rows // (interface // face)
        vm = pl.BlockSpec(memory_space=pltpu.VMEM)
        dma = pltpu.SemaphoreType.DMA
        out = pl.pallas_call(
            functools.partial(kernel, n, doms),
            out_shape=jax.ShapeDtypeStruct((nodes, cols), BF),
            in_specs=[vm, vm, pl.BlockSpec(memory_space=pl.ANY), vm, vm, vm],
            out_specs=vm,
            scratch_shapes=[
                pltpu.VMEM((rows, interface), BF),
                pltpu.VMEM((n, nodes, cols), BF),
                pltpu.VMEM((n, nodes // 128, 128), jnp.int32),
                pltpu.VMEM((interface, cols), F32),
                pltpu.VMEM((interface, cols), BF),
                pltpu.VMEM((interface // 2, face), BF),
                pltpu.VMEM((2 * fr, interface), BF),
                pltpu.VMEM((rows, 2 * face), BF),
                pltpu.VMEM((doms, 3, face, face), BF),
                pltpu.VMEM((doms, 2, face, cols), BF),
                pltpu.VMEM((doms + 1, face, cols), BF),
                pltpu.VMEM((doms + 1, face, cols), BF),
                pltpu.VMEM((doms, face, cols), F32),
                pltpu.VMEM((rows, cols), F32),
                pltpu.VMEM((n, rows, cols), BF),
                pltpu.VMEM((nodes, interface), BF),
                pltpu.VMEM((nodes, nodes), BF),
                pltpu.VMEM((nodes, cols), F32),
                pltpu.VMEM((interface, nodes), BF),
                dma, dma((n,)), dma((n,)), dma((2, n, 2)), dma((n, 2)), dma((n,)), dma((n,)),
                dma((n,)), dma((n,)), dma((2, n, 4)), dma((n, 4)),
                dma((6, doms)), dma((6, doms)), dma((2, doms)), dma((2, doms)),
            ],
            compiler_params=pltpu.CompilerParams(
                collective_id=0, has_side_effects=True, vmem_limit_bytes=60 * 1024 * 1024
            ),
            cost_estimate=pl.CostEstimate(flops=10**10, bytes_accessed=11 * 10**6, transcendentals=0),
        )(
            leaf_map[0, 0], leaf_load[0, 0], group_map[0], node_index.reshape(nodes // 128, 128),
            west_coupling[0], east_coupling[0],
        )
        return out[None, None]

    return jax.shard_map(
        on_device,
        mesh=mesh,
        in_specs=(
            P("dom", "grp", None, None),
            P("dom", "grp", None, None),
            P("dom", "grp", None),
            P("dom", "grp", None),
            P("dom", None, None),
            P("dom", None, None),
        ),
        out_specs=P("dom", "grp", None, None),
        check_vma=False,
    )
```

```python
import functools

import jax
import jax.numpy as jnp
from jax import lax
from jax.experimental import pallas as pl
from jax.experimental.pallas import tpu as pltpu
from jax.sharding import PartitionSpec as P

MESH = pl.DeviceIdType.MESH
BF = jnp.bfloat16
F32 = jnp.float32


def dot(a, b):
    return jnp.dot(a, b, preferred_element_type=F32)


def flip(d, mask):
    out = d
    bit = 1
    while bit <= mask:
        if mask & bit:
            out = out + (1 - 2 * (lax.div(d, bit) % 2)) * bit
        bit *= 2
    return out


def subsets(bits):
    found = [0]
    for bit in bits:
        found += [m | bit for m in found]
    return found


def kernel(
    n, doms,
    lm_ref, ll_ref, g_hbm, idx_ref, wc_ref, ec_ref, out_ref,
    g, contrib, idx_all, loads, loads_b, sel, gface, gsel, maps, faces, ebuf, wbuf, swept, init, sol, pt, lmt, picked, plast,
    g_sem, i_s, i_r, c_s, c_r, m_s, m_r, f_s, f_r, o_s, o_r, ms, mr, fs, fr_,
):
    z = lax.axis_index("grp")
    d = lax.axis_index("dom")
    rows, interface = g.shape
    nodes, cols = ll_ref.shape
    face = wc_ref.shape[0]
    stride = interface // face
    fr = rows // stride
    bits = []
    while (1 << len(bits)) < doms:
        bits.append(1 << len(bits))
    tile = 512

    load_g = pltpu.make_async_copy(g_hbm, g, g_sem)
    load_g.start()
    barrier = pltpu.get_barrier_semaphore()
    for o in range(1, n):
        pl.semaphore_signal(barrier, inc=1, device_id={"grp": (z + o) % n}, device_id_type=MESH)
    for bit in bits:
        pl.semaphore_signal(barrier, inc=1, device_id={"dom": flip(d, bit)}, device_id_type=MESH)

    contrib[z] = dot(lm_ref[...], ll_ref[...]).astype(BF)
    idx_all[z] = idx_ref[...]
    pl.semaphore_wait(barrier, n - 1 + len(bits))

    def to_group(ref, ss, rs):
        made = []
        for o in range(1, n):
            made.append(pltpu.make_async_remote_copy(
                src_ref=ref, dst_ref=ref, send_sem=ss.at[o], recv_sem=rs.at[o],
                device_id={"grp": (z + o) % n}, device_id_type=MESH))
        return made

    def start(copies):
        for c in copies:
            c.start()

    sent = []

    def wait(copies):
        for c in copies:
            c.wait_recv()
        sent.extend(copies)

    can = (z < n - 1, z > 0)

    def have(s, way):
        return z >= s if way == 0 else z + s < n

    def line(part, ss, rs):
        chunks = rs.shape[1]

        def passing(block, c, way):
            ref = part(block, c, chunks)
            return pltpu.make_async_remote_copy(
                src_ref=ref, dst_ref=ref, send_sem=ss.at[way, block, c], recv_sem=rs.at[block, c],
                device_id={"grp": z + 1 - 2 * way}, device_id_type=MESH)

        def move(s):
            for c in range(chunks):
                for way in range(2):
                    block = z - s if way == 0 else z + s
                    if s:
                        @pl.when(have(s, way))
                        def _():
                            passing(block, c, way).wait_recv()

                    @pl.when(jnp.logical_and(have(s, way), can[way]))
                    def _():
                        passing(block, c, way).start()

        def end():
            for s in range(n - 1):
                for c in range(chunks):
                    for way in range(2):
                        block = z - s if way == 0 else z + s

                        @pl.when(jnp.logical_and(have(s, way), can[way]))
                        def _():
                            passing(block, c, way).wait_send()

        return move, end

    def whole_block(buf):
        return lambda block, c, chunks: buf.at[block, pl.ds(c * (buf.shape[1] // chunks), buf.shape[1] // chunks), :]

    def face_block(buf):
        return lambda block, c, chunks: buf.at[d, :, pl.ds(pl.multiple_of(block * fr, fr), fr), :]

    move_contrib, end_contrib = line(whole_block(contrib), c_s, c_r)
    move_sol, end_sol = line(whole_block(sol), o_s, o_r)
    move_maps, end_maps = line(face_block(maps), m_s, m_r)
    move_faces, end_faces = line(face_block(faces), f_s, f_r)
    i_copies = to_group(idx_all.at[z], i_s, i_r)
    start(i_copies)

    half = interface // 2
    hf = face // 2
    a = lax.broadcasted_iota(jnp.int32, (half, face), 0)
    b = lax.broadcasted_iota(jnp.int32, (half, face), 1)
    want = jnp.where(b < hf, b * stride, (b - hf) * stride + 1)
    sel[...] = jnp.where(a == want, 1.0, 0.0).astype(BF)
    a = lax.broadcasted_iota(jnp.int32, (2 * fr, rows), 0)
    b = lax.broadcasted_iota(jnp.int32, (2 * fr, rows), 1)
    want = jnp.where(a < fr, a * stride, (a - fr) * stride + 1)
    pick_rows = jnp.where(b == want, 1.0, 0.0).astype(BF)

    load_g.wait()
    @pl.loop(0, interface // tile)
    def _(i):
        c0 = pl.multiple_of(i * tile, tile)
        gface[:, pl.ds(c0, tile)] = dot(pick_rows, g[:, pl.ds(c0, tile)]).astype(BF)

    got = [dot(gface[:, c * half:(c + 1) * half], sel[...]).astype(BF) for c in range(2)]
    ff = jnp.concatenate([got[0][:, :hf], got[1][:, :hf], got[0][:, hf:], got[1][:, hf:]], axis=1)

    def split(x):
        high = x.astype(BF)
        return high, (x - high.astype(F32)).astype(BF)

    wc_h, wc_l = split(wc_ref[...])
    ec_h, ec_l = split(ec_ref[...])
    forward = dot(ff[:, :face], wc_h) + dot(ff[:, :face], wc_l)
    backward = dot(ff[:fr, face:], ec_h) + dot(ff[:fr, face:], ec_l)
    z0 = pl.multiple_of(z * fr, fr)
    maps[d, 0, pl.ds(z0, fr), :] = forward[:fr].astype(BF)
    maps[d, 1, pl.ds(z0, fr), :] = forward[fr:].astype(BF)
    maps[d, 2, pl.ds(z0, fr), :] = backward.astype(BF)
    move_maps(0)
    move_contrib(0)

    place = lax.broadcasted_iota(jnp.int32, (tile, 128), 0).astype(jnp.int16)

    def one_hot(block, r0):
        made = []
        for r in range(nodes // 128):
            row = jnp.broadcast_to(idx_all[block, pl.ds(r, 1), :] - r0, (16, 128)).astype(jnp.int16)
            row = jnp.concatenate([row] * (tile // 16), axis=0)
            made.append(jnp.where(place == row, jnp.ones((), BF), jnp.zeros((), BF)))
        return jnp.concatenate(made, axis=1)

    upper = 2 * z < n
    near = jnp.where(upper, z, n - 1 - z)

    def arrival(t):
        far = jnp.where(upper, z + (t - near + 1), z - (t - near + 1))
        return jnp.where(t < 2 * near, z + (t // 2 + 1) * (1 - t % 2 * 2), far)

    def add_loads(block, first):
        @pl.loop(0, interface // tile)
        def _(i):
            r0 = pl.multiple_of(i * tile, tile)
            part = dot(one_hot(block, r0), contrib[block])
            if first:
                loads[pl.ds(r0, tile), :] = part
            else:
                loads[pl.ds(r0, tile), :] += part

    def spread(ref, part, order, ss, rs, pick):
        done, steps = [], []
        for bit in order:
            steps.append([pltpu.make_async_remote_copy(
                src_ref=ref.at[flip(d, m), *pick], dst_ref=ref.at[flip(d, m), *pick],
                send_sem=ss.at[part, m | bit], recv_sem=rs.at[part, m | bit],
                device_id={"dom": flip(d, bit)}, device_id_type=MESH) for m in subsets(done)])
            done.append(bit)
        return steps

    order_a = bits[::-1]
    order_b = order_a if len(bits) < 3 else [order_a[1], order_a[0]] + order_a[2:]
    map_steps = [
        spread(maps, p, (order_a, order_b)[p % 2], ms, mr, (p // 2, pl.ds(p % 2 * hf, hf))) for p in range(6)]
    face_steps = [spread(faces, p, (order_a, order_b)[p], fs, fr_, (p,)) for p in range(2)]

    def turn_index():
        turned = jnp.transpose(idx_ref[...])
        for r in range(nodes // 128):
            column = turned[:, r:r + 1]

            @pl.loop(0, interface // tile)
            def _(i):
                c0 = pl.multiple_of(i * tile, tile)
                place = lax.broadcasted_iota(jnp.int32, (128, tile), 1) + c0
                pt[r * 128:(r + 1) * 128, pl.ds(c0, tile)] = jnp.where(place == column, 1.0, 0.0).astype(BF)

    wait(i_copies)
    add_loads(z, True)
    move_maps(1)
    turn_index()
    for s in range(2, n):
        move_maps(s)
    for s in map_steps:
        start(s[0])

    last = arrival(n - 2)
    gp = jnp.zeros((2 * fr, nodes), F32)

    def prepare(i, gp):
        r0 = pl.multiple_of(i * tile, tile)
        hot = one_hot(last, r0)
        plast[pl.ds(r0, tile), :] = hot
        return gp + dot(gface[:, pl.ds(r0, tile)], hot)

    gp = lax.fori_loop(0, interface // tile, prepare, gp).astype(BF)

    if len(bits) > 1:
        for s in map_steps:
            wait(s[0])
            start(s[1])

    for t in range(n - 2):
        move_contrib(t + 1)
        if 1 <= t < len(bits) - 1:
            for s in map_steps:
                wait(s[t])
                start(s[t + 1])
        add_loads(arrival(t), False)
    for k in range(max(n - 1, 2), len(bits)):
        for s in map_steps:
            wait(s[k - 1])
            start(s[k])

    here = dot(gface[...], loads[...].astype(BF))
    move_contrib(n - 1)
    here = (here + dot(gp, contrib[last])).astype(BF)
    faces[d, 0, pl.ds(z0, fr), :] = here[:fr]
    faces[d, 1, pl.ds(z0, fr), :] = here[fr:]
    move_faces(0)

    def end_loads(start, stop):
        @pl.loop(start, stop)
        def _(i):
            r0 = pl.multiple_of(i * tile, tile)
            rest = dot(plast[pl.ds(r0, tile), :], contrib[last])
            loads_b[pl.ds(r0, tile), :] = (loads[pl.ds(r0, tile), :] + rest).astype(BF)

    middle = interface // tile // 2
    end_loads(0, middle)
    move_faces(1)
    end_loads(middle, interface // tile)
    for s in range(2, n):
        move_faces(s)
    for s in face_steps:
        start(s[0])

    step = min(256, rows)

    def take_columns():
        @pl.loop(0, rows // step)
        def _(i):
            r0 = pl.multiple_of(i * step, step)
            for c in range(2):
                got = dot(g[pl.ds(r0, step), c * half:(c + 1) * half], sel[...]).astype(BF)
                gsel[pl.ds(r0, step), c * hf:(c + 1) * hf] = got[:, :hf]
                gsel[pl.ds(r0, step), face + c * hf:face + (c + 1) * hf] = got[:, hf:]

    def start_rows():
        @pl.loop(0, rows // step)
        def _(i):
            r0 = pl.multiple_of(i * step, step)
            init[pl.ds(r0, step), :] = dot(g[pl.ds(r0, step), :], loads_b[...])

    def turn_map():
        lmt[...] = jnp.transpose(lm_ref[...])

    beside = [take_columns, start_rows, turn_map]
    for k in range(1, len(bits)):
        if beside:
            beside.pop(0)()
        for s in face_steps:
            wait(s[k - 1])
            start(s[k])
    for work in beside:
        work()
    for s in map_steps:
        wait(s[-1])
    for s in face_steps:
        wait(s[-1])

    ebuf[0] = jnp.zeros((face, cols), BF)
    east = faces[0, 1]
    ebuf[1] = east
    for j in range(1, doms):
        swept[j] = dot(maps[j, 0], east) + faces[j, 0].astype(F32)
        if j < doms - 1:
            east = (dot(maps[j, 1], east) + faces[j, 1].astype(F32)).astype(BF)
            ebuf[j + 1] = east
    wbuf[doms] = jnp.zeros((face, cols), BF)
    west = swept[doms - 1].astype(BF)
    wbuf[doms - 1] = west
    for j in range(doms - 2, 0, -1):
        west = (swept[j] + dot(maps[j, 2], west)).astype(BF)
        wbuf[j] = west
    inc = ebuf[d]
    outgoing = wbuf[d + 1]
    vw = (dot(wc_h, inc) + dot(wc_l, inc)).astype(BF)
    ve = (dot(ec_h, outgoing) + dot(ec_l, outgoing)).astype(BF)
    sol[z] = (init[...] + dot(gsel[...], jnp.concatenate([vw, ve], axis=0))).astype(BF)
    def add_picked(block):
        c0 = pl.multiple_of(block * rows, rows)
        return dot(pt[:, pl.ds(c0, rows)], sol[block])

    for s in range(n):
        move_sol(s)
        if s == 0:
            picked[...] = add_picked(z)
            continue
        for way in range(2):
            block = z - s if way == 0 else z + s

            @pl.when(have(s, way))
            def _():
                picked[...] += add_picked(block)

    for c in sent:
        c.wait_send()
    end_contrib()
    end_maps()
    end_faces()
    end_sol()

    out_ref[...] = (dot(lmt[...], picked[...].astype(BF)) + ll_ref[...].astype(F32)).astype(BF)


def solution(mesh):
    n, doms = mesh.shape["grp"], mesh.shape["dom"]

    def on_device(leaf_load, leaf_map, group_map, node_index, west_coupling, east_coupling):
        nodes, cols = leaf_load.shape[2:]
        rows, interface = group_map.shape[1:]
        face = west_coupling.shape[1]
        fr = rows // (interface // face)
        vm = pl.BlockSpec(memory_space=pltpu.VMEM)
        dma = pltpu.SemaphoreType.DMA
        out = pl.pallas_call(
            functools.partial(kernel, n, doms),
            out_shape=jax.ShapeDtypeStruct((nodes, cols), BF),
            in_specs=[vm, vm, pl.BlockSpec(memory_space=pl.ANY), vm, vm, vm],
            out_specs=vm,
            scratch_shapes=[
                pltpu.VMEM((rows, interface), BF),
                pltpu.VMEM((n, nodes, cols), BF),
                pltpu.VMEM((n, nodes // 128, 128), jnp.int32),
                pltpu.VMEM((interface, cols), F32),
                pltpu.VMEM((interface, cols), BF),
                pltpu.VMEM((interface // 2, face), BF),
                pltpu.VMEM((2 * fr, interface), BF),
                pltpu.VMEM((rows, 2 * face), BF),
                pltpu.VMEM((doms, 3, face, face), BF),
                pltpu.VMEM((doms, 2, face, cols), BF),
                pltpu.VMEM((doms + 1, face, cols), BF),
                pltpu.VMEM((doms + 1, face, cols), BF),
                pltpu.VMEM((doms, face, cols), F32),
                pltpu.VMEM((rows, cols), F32),
                pltpu.VMEM((n, rows, cols), BF),
                pltpu.VMEM((nodes, interface), BF),
                pltpu.VMEM((nodes, nodes), BF),
                pltpu.VMEM((nodes, cols), F32),
                pltpu.VMEM((interface, nodes), BF),
                dma, dma((n,)), dma((n,)), dma((2, n, 2)), dma((n, 2)), dma((2, n, 1)), dma((n, 1)),
                dma((2, n, 1)), dma((n, 1)), dma((2, n, 4)), dma((n, 4)),
                dma((6, doms)), dma((6, doms)), dma((2, doms)), dma((2, doms)),
            ],
            compiler_params=pltpu.CompilerParams(
                collective_id=0, has_side_effects=True, vmem_limit_bytes=60 * 1024 * 1024
            ),
            cost_estimate=pl.CostEstimate(flops=10**10, bytes_accessed=11 * 10**6, transcendentals=0),
        )(
            leaf_map[0, 0], leaf_load[0, 0], group_map[0], node_index.reshape(nodes // 128, 128),
            west_coupling[0], east_coupling[0],
        )
        return out[None, None]

    return jax.shard_map(
        on_device,
        mesh=mesh,
        in_specs=(
            P("dom", "grp", None, None),
            P("dom", "grp", None, None),
            P("dom", "grp", None),
            P("dom", "grp", None),
            P("dom", None, None),
            P("dom", None, None),
        ),
        out_specs=P("dom", "grp", None, None),
        check_vma=False,
    )
```

```python
import functools

import jax
import jax.numpy as jnp
from jax import lax
from jax.experimental import pallas as pl
from jax.experimental.pallas import tpu as pltpu
from jax.sharding import PartitionSpec as P

MESH = pl.DeviceIdType.MESH
BF = jnp.bfloat16
F32 = jnp.float32


def dot(a, b):
    return jnp.dot(a, b, preferred_element_type=F32)


def flip(d, mask):
    out = d
    bit = 1
    while bit <= mask:
        if mask & bit:
            out = out + (1 - 2 * (lax.div(d, bit) % 2)) * bit
        bit *= 2
    return out


def subsets(bits):
    found = [0]
    for bit in bits:
        found += [m | bit for m in found]
    return found


def kernel(
    n, doms,
    lm_ref, ll_ref, g_hbm, idx_ref, wc_ref, ec_ref, out_ref,
    g, contrib, idx_all, loads, loads_b, sel, gface, gsel, maps, faces, ebuf, wbuf, swept, init, sol, pt, lmt, picked, plast,
    g_sem, i_s, i_r, c_s, c_r, m_s, m_r, f_s, f_r, o_s, o_r, ms, mr, fs, fr_,
):
    z = lax.axis_index("grp")
    d = lax.axis_index("dom")
    rows, interface = g.shape
    nodes, cols = ll_ref.shape
    face = wc_ref.shape[0]
    stride = interface // face
    fr = rows // stride
    bits = []
    while (1 << len(bits)) < doms:
        bits.append(1 << len(bits))
    tile = 512

    load_g = pltpu.make_async_copy(g_hbm, g, g_sem)
    load_g.start()
    barrier = pltpu.get_barrier_semaphore()
    for o in range(1, n):
        pl.semaphore_signal(barrier, inc=1, device_id={"grp": (z + o) % n}, device_id_type=MESH)
    for bit in bits:
        pl.semaphore_signal(barrier, inc=1, device_id={"dom": flip(d, bit)}, device_id_type=MESH)

    contrib[z] = dot(lm_ref[...], ll_ref[...]).astype(BF)
    idx_all[z] = idx_ref[...]
    pl.semaphore_wait(barrier, n - 1 + len(bits))

    def to_group(ref, ss, rs):
        made = []
        for o in range(1, n):
            made.append(pltpu.make_async_remote_copy(
                src_ref=ref, dst_ref=ref, send_sem=ss.at[o], recv_sem=rs.at[o],
                device_id={"grp": (z + o) % n}, device_id_type=MESH))
        return made

    def start(copies):
        for c in copies:
            c.start()

    sent = []

    def wait(copies):
        for c in copies:
            c.wait_recv()
        sent.extend(copies)

    can = (z < n - 1, z > 0)

    def have(s, way):
        return z >= s if way == 0 else z + s < n

    def line(buf, ss, rs):
        chunks = rs.shape[1]
        span = buf.shape[1] // chunks

        def passing(block, c, way):
            ref = buf.at[block, pl.ds(c * span, span), :]
            return pltpu.make_async_remote_copy(
                src_ref=ref, dst_ref=ref, send_sem=ss.at[way, block, c], recv_sem=rs.at[block, c],
                device_id={"grp": z + 1 - 2 * way}, device_id_type=MESH)

        def move(s):
            for c in range(chunks):
                for way in range(2):
                    block = z - s if way == 0 else z + s
                    if s:
                        @pl.when(have(s, way))
                        def _():
                            passing(block, c, way).wait_recv()

                    @pl.when(jnp.logical_and(have(s, way), can[way]))
                    def _():
                        passing(block, c, way).start()

        def end():
            for s in range(n - 1):
                for c in range(chunks):
                    for way in range(2):
                        block = z - s if way == 0 else z + s

                        @pl.when(jnp.logical_and(have(s, way), can[way]))
                        def _():
                            passing(block, c, way).wait_send()

        return move, end

    move_contrib, end_contrib = line(contrib, c_s, c_r)
    move_sol, end_sol = line(sol, o_s, o_r)
    i_copies = to_group(idx_all.at[z], i_s, i_r)
    start(i_copies)

    half = interface // 2
    hf = face // 2
    a = lax.broadcasted_iota(jnp.int32, (half, face), 0)
    b = lax.broadcasted_iota(jnp.int32, (half, face), 1)
    want = jnp.where(b < hf, b * stride, (b - hf) * stride + 1)
    sel[...] = jnp.where(a == want, 1.0, 0.0).astype(BF)
    a = lax.broadcasted_iota(jnp.int32, (2 * fr, rows), 0)
    b = lax.broadcasted_iota(jnp.int32, (2 * fr, rows), 1)
    want = jnp.where(a < fr, a * stride, (a - fr) * stride + 1)
    pick_rows = jnp.where(b == want, 1.0, 0.0).astype(BF)

    load_g.wait()
    @pl.loop(0, interface // tile)
    def _(i):
        c0 = pl.multiple_of(i * tile, tile)
        gface[:, pl.ds(c0, tile)] = dot(pick_rows, g[:, pl.ds(c0, tile)]).astype(BF)

    got = [dot(gface[:, c * half:(c + 1) * half], sel[...]).astype(BF) for c in range(2)]
    ff = jnp.concatenate([got[0][:, :hf], got[1][:, :hf], got[0][:, hf:], got[1][:, hf:]], axis=1)

    def split(x):
        high = x.astype(BF)
        return high, (x - high.astype(F32)).astype(BF)

    wc_h, wc_l = split(wc_ref[...])
    ec_h, ec_l = split(ec_ref[...])
    forward = dot(ff[:, :face], wc_h) + dot(ff[:, :face], wc_l)
    backward = dot(ff[:fr, face:], ec_h) + dot(ff[:fr, face:], ec_l)
    z0 = pl.multiple_of(z * fr, fr)
    maps[d, 0, pl.ds(z0, fr), :] = forward[:fr].astype(BF)
    maps[d, 1, pl.ds(z0, fr), :] = forward[fr:].astype(BF)
    maps[d, 2, pl.ds(z0, fr), :] = backward.astype(BF)
    m_copies = to_group(maps.at[d, :, pl.ds(z0, fr), :], m_s, m_r)
    start(m_copies)

    move_contrib(0)

    place = lax.broadcasted_iota(jnp.int32, (tile, 128), 0).astype(jnp.int16)

    def one_hot(block, r0):
        made = []
        for r in range(nodes // 128):
            row = jnp.broadcast_to(idx_all[block, pl.ds(r, 1), :] - r0, (16, 128)).astype(jnp.int16)
            row = jnp.concatenate([row] * (tile // 16), axis=0)
            made.append(jnp.where(place == row, jnp.ones((), BF), jnp.zeros((), BF)))
        return jnp.concatenate(made, axis=1)

    upper = 2 * z < n
    near = jnp.where(upper, z, n - 1 - z)

    def arrival(t):
        far = jnp.where(upper, z + (t - near + 1), z - (t - near + 1))
        return jnp.where(t < 2 * near, z + (t // 2 + 1) * (1 - t % 2 * 2), far)

    def add_loads(block, first):
        @pl.loop(0, interface // tile)
        def _(i):
            r0 = pl.multiple_of(i * tile, tile)
            part = dot(one_hot(block, r0), contrib[block])
            if first:
                loads[pl.ds(r0, tile), :] = part
            else:
                loads[pl.ds(r0, tile), :] += part

    def spread(ref, part, order, ss, rs, pick):
        done, steps = [], []
        for bit in order:
            steps.append([pltpu.make_async_remote_copy(
                src_ref=ref.at[flip(d, m), *pick], dst_ref=ref.at[flip(d, m), *pick],
                send_sem=ss.at[part, m | bit], recv_sem=rs.at[part, m | bit],
                device_id={"dom": flip(d, bit)}, device_id_type=MESH) for m in subsets(done)])
            done.append(bit)
        return steps

    order_a = bits[::-1]
    order_b = order_a if len(bits) < 3 else [order_a[1], order_a[0]] + order_a[2:]
    map_steps = [
        spread(maps, p, (order_a, order_b)[p % 2], ms, mr, (p // 2, pl.ds(p % 2 * hf, hf))) for p in range(6)]
    face_steps = [spread(faces, p, (order_a, order_b)[p], fs, fr_, (p,)) for p in range(2)]

    def turn_index():
        turned = jnp.transpose(idx_ref[...])
        for r in range(nodes // 128):
            column = turned[:, r:r + 1]

            @pl.loop(0, interface // tile)
            def _(i):
                c0 = pl.multiple_of(i * tile, tile)
                place = lax.broadcasted_iota(jnp.int32, (128, tile), 1) + c0
                pt[r * 128:(r + 1) * 128, pl.ds(c0, tile)] = jnp.where(place == column, 1.0, 0.0).astype(BF)

    wait(i_copies)
    add_loads(z, True)
    turn_index()
    wait(m_copies)
    for s in map_steps:
        start(s[0])

    last = arrival(n - 2)
    gp = jnp.zeros((2 * fr, nodes), F32)

    def prepare(i, gp):
        r0 = pl.multiple_of(i * tile, tile)
        hot = one_hot(last, r0)
        plast[pl.ds(r0, tile), :] = hot
        return gp + dot(gface[:, pl.ds(r0, tile)], hot)

    gp = lax.fori_loop(0, interface // tile, prepare, gp).astype(BF)

    if len(bits) > 1:
        for s in map_steps:
            wait(s[0])
            start(s[1])

    for t in range(n - 2):
        move_contrib(t + 1)
        if 1 <= t < len(bits) - 1:
            for s in map_steps:
                wait(s[t])
                start(s[t + 1])
        add_loads(arrival(t), False)
    for k in range(max(n - 1, 2), len(bits)):
        for s in map_steps:
            wait(s[k - 1])
            start(s[k])

    here = dot(gface[...], loads[...].astype(BF))
    move_contrib(n - 1)
    here = (here + dot(gp, contrib[last])).astype(BF)
    faces[d, 0, pl.ds(z0, fr), :] = here[:fr]
    faces[d, 1, pl.ds(z0, fr), :] = here[fr:]
    f_copies = to_group(faces.at[d, :, pl.ds(z0, fr), :], f_s, f_r)
    start(f_copies)

    @pl.loop(0, interface // tile)
    def _(i):
        r0 = pl.multiple_of(i * tile, tile)
        loads_b[pl.ds(r0, tile), :] = (loads[pl.ds(r0, tile), :] + dot(plast[pl.ds(r0, tile), :], contrib[last])).astype(BF)

    wait(f_copies)
    for s in face_steps:
        start(s[0])

    step = min(256, rows)

    def take_columns():
        @pl.loop(0, rows // step)
        def _(i):
            r0 = pl.multiple_of(i * step, step)
            for c in range(2):
                got = dot(g[pl.ds(r0, step), c * half:(c + 1) * half], sel[...]).astype(BF)
                gsel[pl.ds(r0, step), c * hf:(c + 1) * hf] = got[:, :hf]
                gsel[pl.ds(r0, step), face + c * hf:face + (c + 1) * hf] = got[:, hf:]

    def start_rows():
        @pl.loop(0, rows // step)
        def _(i):
            r0 = pl.multiple_of(i * step, step)
            init[pl.ds(r0, step), :] = dot(g[pl.ds(r0, step), :], loads_b[...])

    def turn_map():
        lmt[...] = jnp.transpose(lm_ref[...])

    beside = [take_columns, start_rows, turn_map]
    for k in range(1, len(bits)):
        if beside:
            beside.pop(0)()
        for s in face_steps:
            wait(s[k - 1])
            start(s[k])
    for work in beside:
        work()
    for s in map_steps:
        wait(s[-1])
    for s in face_steps:
        wait(s[-1])

    ebuf[0] = jnp.zeros((face, cols), BF)
    east = faces[0, 1]
    ebuf[1] = east
    for j in range(1, doms):
        swept[j] = dot(maps[j, 0], east) + faces[j, 0].astype(F32)
        if j < doms - 1:
            east = (dot(maps[j, 1], east) + faces[j, 1].astype(F32)).astype(BF)
            ebuf[j + 1] = east
    wbuf[doms] = jnp.zeros((face, cols), BF)
    west = swept[doms - 1].astype(BF)
    wbuf[doms - 1] = west
    for j in range(doms - 2, 0, -1):
        west = (swept[j] + dot(maps[j, 2], west)).astype(BF)
        wbuf[j] = west
    inc = ebuf[d]
    outgoing = wbuf[d + 1]
    vw = (dot(wc_h, inc) + dot(wc_l, inc)).astype(BF)
    ve = (dot(ec_h, outgoing) + dot(ec_l, outgoing)).astype(BF)
    sol[z] = (init[...] + dot(gsel[...], jnp.concatenate([vw, ve], axis=0))).astype(BF)
    def add_picked(block):
        c0 = pl.multiple_of(block * rows, rows)
        return dot(pt[:, pl.ds(c0, rows)], sol[block])

    for s in range(n):
        move_sol(s)
        if s == 0:
            picked[...] = add_picked(z)
            continue
        for way in range(2):
            block = z - s if way == 0 else z + s

            @pl.when(have(s, way))
            def _():
                picked[...] += add_picked(block)

    for c in sent:
        c.wait_send()
    end_contrib()
    end_sol()

    out_ref[...] = (dot(lmt[...], picked[...].astype(BF)) + ll_ref[...].astype(F32)).astype(BF)


def solution(mesh):
    n, doms = mesh.shape["grp"], mesh.shape["dom"]

    def on_device(leaf_load, leaf_map, group_map, node_index, west_coupling, east_coupling):
        nodes, cols = leaf_load.shape[2:]
        rows, interface = group_map.shape[1:]
        face = west_coupling.shape[1]
        fr = rows // (interface // face)
        vm = pl.BlockSpec(memory_space=pltpu.VMEM)
        dma = pltpu.SemaphoreType.DMA
        out = pl.pallas_call(
            functools.partial(kernel, n, doms),
            out_shape=jax.ShapeDtypeStruct((nodes, cols), BF),
            in_specs=[vm, vm, pl.BlockSpec(memory_space=pl.ANY), vm, vm, vm],
            out_specs=vm,
            scratch_shapes=[
                pltpu.VMEM((rows, interface), BF),
                pltpu.VMEM((n, nodes, cols), BF),
                pltpu.VMEM((n, nodes // 128, 128), jnp.int32),
                pltpu.VMEM((interface, cols), F32),
                pltpu.VMEM((interface, cols), BF),
                pltpu.VMEM((interface // 2, face), BF),
                pltpu.VMEM((2 * fr, interface), BF),
                pltpu.VMEM((rows, 2 * face), BF),
                pltpu.VMEM((doms, 3, face, face), BF),
                pltpu.VMEM((doms, 2, face, cols), BF),
                pltpu.VMEM((doms + 1, face, cols), BF),
                pltpu.VMEM((doms + 1, face, cols), BF),
                pltpu.VMEM((doms, face, cols), F32),
                pltpu.VMEM((rows, cols), F32),
                pltpu.VMEM((n, rows, cols), BF),
                pltpu.VMEM((nodes, interface), BF),
                pltpu.VMEM((nodes, nodes), BF),
                pltpu.VMEM((nodes, cols), F32),
                pltpu.VMEM((interface, nodes), BF),
                dma, dma((n,)), dma((n,)), dma((2, n, 4)), dma((n, 4)), dma((n,)), dma((n,)),
                dma((n,)), dma((n,)), dma((2, n, 4)), dma((n, 4)),
                dma((6, doms)), dma((6, doms)), dma((2, doms)), dma((2, doms)),
            ],
            compiler_params=pltpu.CompilerParams(
                collective_id=0, has_side_effects=True, vmem_limit_bytes=60 * 1024 * 1024
            ),
            cost_estimate=pl.CostEstimate(flops=10**10, bytes_accessed=11 * 10**6, transcendentals=0),
        )(
            leaf_map[0, 0], leaf_load[0, 0], group_map[0], node_index.reshape(nodes // 128, 128),
            west_coupling[0], east_coupling[0],
        )
        return out[None, None]

    return jax.shard_map(
        on_device,
        mesh=mesh,
        in_specs=(
            P("dom", "grp", None, None),
            P("dom", "grp", None, None),
            P("dom", "grp", None),
            P("dom", "grp", None),
            P("dom", None, None),
            P("dom", None, None),
        ),
        out_specs=P("dom", "grp", None, None),
        check_vma=False,
    )
```
